32 devices in a mesh: dp: 2 (over x), seq: 16 (over z, y, core).
Axes of the slice: x: 2, y: 2, z: 4, core: 2. Of those that a mesh axis runs over, the one named last changes fastest.
Arguments:
- inputs: float32 [2, 2048, 128], P('dp', 'seq'), parts along dimension 0, may hold values from -48 to 48
- trajectory: float32 [2, 2048, 128], P('dp', 'seq'), parts along dimension 0, may hold values from -0.9 to 0.9
- initial_state: float32 [2, 128], P('dp'), parts along dimension 0, may hold values from -0.9 to 0.9
- cotangent: float32 [2, 2048, 128], P('dp', 'seq'), parts along dimension 0, may hold values from -1 to 1
- in_weight: float32 [128, 384], replicated, may hold values from -0.5 to 0.5
- recurrent_weight: float32 [128, 384], replicated, may hold values from -0.5 to 0.5
- gate_bias: float32 [384], replicated
Outputs:
- new_state: float32 [2, 2048, 128], P('dp', 'seq'), parts along dimension 0
- adjoint: float32 [2, 2048, 128], P('dp', 'seq'), parts along dimension 0
The draws below stay inside these ranges and needn't reach their ends.
There are 2 independent parts, one for each index of `dp`. The reference program is written for one: setup_inputs(seed, part) draws one part's arguments, and reference() takes and returns one part's arrays. A program takes and returns all parts, laid end to end along the dimension named above; an argument that names none is the same for every part. Nothing has to cross between parts.
All inputs are finite; a program needn't handle non-finite values.
Results may differ from the reference program's by a relative error of at most 0.0003.
Values sent between devices are 32-bit elements; how exact they have to be, the bound alone decides.
A program may use at most 64 MiB of HBM per device.

```python
import math
import jax
import jax.numpy as jnp
from jax import lax

H = 128
D_IN = 128
TOKENS = 2048


def draw_inputs(key, part):
    first_key, second_key = jax.random.split(key, 2)
    shape = (1, TOKENS, D_IN)
    starting_level = jnp.clip(jax.random.normal(first_key, shape, jnp.float32), -4.0, 4.0)
    picked_locations = jax.random.randint(second_key, (4,), 0, TOKENS)
    linear_map_lines = lax.broadcasted_iota(jnp.int32, (1, TOKENS, 1), 1)
    contiguous_span = jnp.any(linear_map_lines == picked_locations, axis=-1, keepdims=True)
    weighted_summand = starting_level * jnp.where(contiguous_span, 12.0, 1.0)
    return weighted_summand.astype(jnp.float32)


def draw_cotangent(key, part):
    shape = (1, TOKENS, H)
    factor = 2.0 / math.sqrt(TOKENS)
    starting_level = jnp.clip(jax.random.normal(key, shape, jnp.float32), -4.0, 4.0)
    return (starting_level * factor).astype(jnp.float32)


def draw_gate_bias(key, part):
    first_key, second_key, third_key, fourth_key = jax.random.split(key, 4)
    shuffled = jax.random.permutation(first_key, H)
    slow_count = H // 2
    slow_rows = shuffled < slow_count
    slow_bias = -(math.log(TOKENS) + 1.5) + jax.random.uniform(second_key, (H,), jnp.float32, -0.5, 0.5)
    fast_bias = -jax.random.uniform(third_key, (H,), jnp.float32, math.log(30.0), math.log(50.0))
    write_bias = jnp.where(slow_rows, slow_bias, fast_bias)
    others = jax.random.uniform(fourth_key, (2, H), jnp.float32, -1.0, 1.0)
    return jnp.concatenate([others[0], write_bias, others[1]]).astype(jnp.float32)


def steps_of(own_key, dims, cuts, smallest, largest):
    def one(axis_at, blocks):
        heights = jax.random.uniform(jax.random.fold_in(jax.random.fold_in(own_key, 6), axis_at), (blocks,), jnp.float32, smallest / len(cuts), largest / len(cuts))
        return jnp.repeat(jnp.exp(heights), dims[axis_at] // blocks).reshape((-1,) + (1,) * (len(dims) - axis_at - 1))

    gain = one(*cuts[0])
    for cut in cuts[1:]:
        gain = gain * one(*cut)
    return gain


def scatter_about(own_key, shape, deviation, reach, held_as=jnp.bfloat16):
    return jnp.clip(deviation * jax.random.normal(own_key, shape, jnp.float32), -reach, reach).astype(held_as)


def setup_inputs(seed: int = 0, part: int = 0) -> dict:
    key_of = jax.random.split(jax.random.key(seed), 8)
    part_splits = jax.random.split(jax.random.fold_in(key_of[7], part), 8)
    inputs = draw_inputs(jax.random.fold_in(jax.random.fold_in(key_of[7], part), 71), part)
    trajectory = jnp.clip(jax.random.uniform(part_splits[1], (1, TOKENS, H), jnp.float32, -0.9, 0.9) * steps_of(part_splits[1], (1, TOKENS, H), ((1, 16),), -0.4, 0.0), -0.9, 0.9)
    initial_state = jnp.clip(jax.random.uniform(part_splits[2], (1, H), jnp.float32, -0.9, 0.9), -0.9, 0.9)
    cotangent = draw_cotangent(jax.random.fold_in(jax.random.fold_in(key_of[7], part), 71), part)
    in_weight = scatter_about(key_of[4], (D_IN, 3 * H), D_IN ** -0.5, 0.5, jnp.float32)
    recurrent_weight = scatter_about(key_of[5], (H, 3 * H), H ** -0.5, 0.5, jnp.float32)
    gate_bias = draw_gate_bias(jax.random.fold_in(key_of[7], 71), part)
    return dict(inputs=inputs, trajectory=trajectory, initial_state=initial_state, cotangent=cotangent, in_weight=in_weight, recurrent_weight=recurrent_weight, gate_bias=gate_bias)


HIGHEST_PRECISION = lax.Precision.HIGHEST


def sum_parts(tensor, hidden_width):
    return tensor[..., :hidden_width] + tensor[..., hidden_width:2 * hidden_width] + tensor[..., 2 * hidden_width:]


def linearize(features, previous, in_weight, recurrent_weight, gate_bias):
    hidden_width = previous.shape[-1]
    projected = jnp.dot(features, in_weight, precision=HIGHEST_PRECISION, preferred_element_type=jnp.float32) + gate_bias
    recurrent = jnp.dot(previous, recurrent_weight, precision=HIGHEST_PRECISION, preferred_element_type=jnp.float32)
    reset_gate = jax.nn.sigmoid(projected[:, :hidden_width] + recurrent[:, :hidden_width])
    write_gate = jax.nn.sigmoid(projected[:, hidden_width:2 * hidden_width] + recurrent[:, hidden_width:2 * hidden_width])
    cand_recurrent = recurrent[:, 2 * hidden_width:]
    candidate = jnp.tanh(projected[:, 2 * hidden_width:] + reset_gate * cand_recurrent)
    updated = previous + write_gate * (candidate - previous)
    keep_rate = 1.0 - write_gate
    slopes = write_gate * (1.0 - candidate * candidate)
    gate_terms = jnp.concatenate([slopes * cand_recurrent * reset_gate * (1.0 - reset_gate), (candidate - previous) * write_gate * (1.0 - write_gate), slopes * reset_gate], axis=1)
    offsets = updated - keep_rate * previous - sum_parts(gate_terms * recurrent, hidden_width)
    return keep_rate, gate_terms, offsets


def apply_jacobian(keep_rate, gate_terms, vector, recurrent_weight):
    hidden_width = vector.shape[-1]
    mapped = jnp.einsum('bk,kj->bj', vector, recurrent_weight, precision=HIGHEST_PRECISION)
    return keep_rate * vector + sum_parts(gate_terms * mapped, hidden_width)


def apply_transposed(keep_rate, gate_terms, vector, recurrent_weight):
    tiled = jnp.concatenate([vector, vector, vector], axis=-1)
    return keep_rate * vector + jnp.einsum('bk,jk->bj', gate_terms * tiled, recurrent_weight, precision=HIGHEST_PRECISION)


def reference(inputs, trajectory, initial_state, cotangent, in_weight, recurrent_weight, gate_bias):
    path = trajectory[0]
    previous = jnp.concatenate([initial_state, path[:-1]], axis=0)
    keep_rate, gate_terms, offsets = linearize(inputs[0], previous, in_weight, recurrent_weight, gate_bias)

    def forward(hidden_state, step_items):
        keep_now, terms_now, offset_now = step_items
        hidden_state = apply_jacobian(keep_now[None], terms_now[None], hidden_state[None], recurrent_weight)[0] + offset_now
        return hidden_state, hidden_state

    _, states = lax.scan(forward, initial_state[0], (keep_rate, gate_terms, offsets))

    def backward(carried, step_items):
        keep_now, terms_now, cotan_now = step_items
        costate = cotan_now + carried
        carried = apply_transposed(keep_now[None], terms_now[None], costate[None], recurrent_weight)[0]
        return carried, costate

    start_adjoint = jnp.zeros((path.shape[1],), jnp.float32)
    _, adjoint_rows = lax.scan(backward, start_adjoint, (keep_rate, gate_terms, cotangent[0]), reverse=True)
    return states[None], adjoint_rows[None]
```

```python
import functools

import jax
import jax.numpy as jnp
from jax import lax
from jax.experimental import pallas as pl
from jax.experimental.pallas import tpu as pltpu
from jax.sharding import PartitionSpec as P

BLOCK = 8
GROUP_LEVELS = (1, 2)
GROUP = 4
PAD = 16

HIGHEST_PRECISION = lax.Precision.HIGHEST
NT = (((1,), (1,)), ((), ()))
NN = (((1,), (0,)), ((), ()))


def split(value):
    high = value.astype(jnp.bfloat16)
    low = (value - high.astype(jnp.float32)).astype(jnp.bfloat16)
    return high, low


def product(rows, weights):
    high, low = split(rows)
    w_high, w_low = split(weights)
    width = weights.shape[1]
    stacked = jnp.concatenate(
        [
            jnp.concatenate([w_high, w_low], axis=1),
            jnp.concatenate([w_high, jnp.zeros_like(w_low)], axis=1),
        ],
        axis=0,
    )
    out = jnp.dot(
        jnp.concatenate([high, low], axis=1), stacked, preferred_element_type=jnp.float32
    )
    return out[:, :width] + out[:, width:]


def few_rows(rows, w_high, w_low, dims):
    high, low = split(rows)
    count = rows.shape[0]
    both = lax.dot_general(
        jnp.concatenate([high, low], axis=0), w_high, dims, preferred_element_type=jnp.float32
    )
    extra = lax.dot_general(high, w_low, dims, preferred_element_type=jnp.float32)
    return both[:count] + both[count:] + extra


def row_sums(matrix):
    high, low = split(matrix)
    ones = jnp.ones((PAD, matrix.shape[1]), jnp.bfloat16)
    total = lax.dot_general(ones, high, NT, preferred_element_type=jnp.float32)
    return total + lax.dot_general(ones, low, NT, preferred_element_type=jnp.float32)


def merge(early, late):
    early_map, early_adjoint = early
    late_map, late_adjoint = late
    width = early_map.shape[1]
    merged = product(early_map, late_map[:width])
    merged = jnp.concatenate([merged[:width], merged[width:] + late_map[width:]], axis=0)
    high, low = split(early_map[:width])
    adjoint = early_adjoint + few_rows(late_adjoint, high, low, NT)
    return merged, adjoint


def go_forward(node, state):
    mapped, _ = node
    width = mapped.shape[1]
    high, low = split(mapped[:width])
    return few_rows(state, high, low, NN) + mapped[width:]


def go_back(node, costate):
    mapped, adjoint = node
    width = mapped.shape[1]
    high, low = split(mapped[:width])
    return few_rows(costate, high, low, NT) + adjoint


def kernel(
    seq_count,
    features_ref,
    path_ref,
    initial_ref,
    cotan_ref,
    in_weight_ref,
    weight_ref,
    bias_ref,
    state_out,
    adjoint_out,
    previous_ref,
    keep_ref,
    term_ref,
    offset_ref,
    map_ref,
    acc_ref,
    pair_ref,
    row_ref,
    ahead_ref,
    behind_ref,
    out_ahead_ref,
    out_behind_ref,
    row_sems,
    pair_send,
    pair_recv,
    ahead_sems,
    behind_sems,
):
    rows, width = path_ref.shape
    blocks = rows // BLOCK
    me = lax.axis_index("seq")
    groups = seq_count // GROUP
    group = me // GROUP

    def at(place):
        return {"seq": place}

    barrier = pltpu.get_barrier_semaphore()
    greeted = jnp.int32(0)
    for distance in (1, GROUP):

        @pl.when(me >= distance)
        def _():
            pl.semaphore_signal(barrier, inc=1, device_id=at(me - distance))

        @pl.when(me < seq_count - distance)
        def _():
            pl.semaphore_signal(barrier, inc=1, device_id=at(me + distance))

        greeted = greeted + jnp.where(me >= distance, 1, 0)
        greeted = greeted + jnp.where(me < seq_count - distance, 1, 0)
    sides = [(me // bit) % 2 for bit in GROUP_LEVELS]
    partners = [me + bit - 2 * bit * side for bit, side in zip(GROUP_LEVELS, sides)]
    for partner in partners[1:]:
        pl.semaphore_signal(barrier, inc=1, device_id=at(partner))
        greeted = greeted + 1
    pl.semaphore_wait(barrier, greeted)

    row_copy = pltpu.make_async_remote_copy(
        src_ref=path_ref.at[pl.ds(rows - 8, 8)],
        dst_ref=row_ref,
        send_sem=row_sems.at[0],
        recv_sem=row_sems.at[1],
        device_id=at(me + 1),
    )

    @pl.when(me < seq_count - 1)
    def _():
        row_copy.start()

    projected = (
        jnp.dot(
            features_ref[...],
            in_weight_ref[...],
            precision=HIGHEST_PRECISION,
            preferred_element_type=jnp.float32,
        )
        + bias_ref[...]
    )
    previous_ref[pl.ds(1, rows - 1), :] = path_ref[pl.ds(0, rows - 1), :]

    @pl.when(me > 0)
    def _():
        row_copy.wait_recv()
        previous_ref[pl.ds(0, 1), :] = row_ref[pl.ds(7, 1), :]

    @pl.when(me == 0)
    def _():
        previous_ref[pl.ds(0, 1), :] = initial_ref[...]

    previous = previous_ref[...]
    recurrent = jnp.dot(
        previous,
        weight_ref[...],
        precision=HIGHEST_PRECISION,
        preferred_element_type=jnp.float32,
    )
    reset_gate = jax.nn.sigmoid(projected[:, :width] + recurrent[:, :width])
    write_gate = jax.nn.sigmoid(
        projected[:, width : 2 * width] + recurrent[:, width : 2 * width]
    )
    cand_recurrent = recurrent[:, 2 * width :]
    candidate = jnp.tanh(projected[:, 2 * width :] + reset_gate * cand_recurrent)
    updated = previous + write_gate * (candidate - previous)
    keep_rate = 1.0 - write_gate
    slopes = write_gate * (1.0 - candidate * candidate)
    reset_terms = slopes * cand_recurrent * reset_gate * (1.0 - reset_gate)
    write_terms = (candidate - previous) * write_gate * (1.0 - write_gate)
    cand_terms = slopes * reset_gate
    keep_ref[...] = keep_rate
    term_ref[0] = reset_terms
    term_ref[1] = write_terms
    term_ref[2] = cand_terms
    offset_ref[...] = (
        updated
        - keep_rate * previous
        - reset_terms * recurrent[:, :width]
        - write_terms * recurrent[:, width : 2 * width]
        - cand_terms * cand_recurrent
    )

    def coupling(row):
        total = weight_ref[:, pl.ds(0, width)] * term_ref[0, pl.ds(row, 1), :]
        for part in (1, 2):
            columns = pl.ds(part * width, width)
            total = total + weight_ref[:, columns] * term_ref[part, pl.ds(row, 1), :]
        return total

    diagonal = lax.broadcasted_iota(jnp.int32, (width, width), 0) == lax.broadcasted_iota(
        jnp.int32, (width, width), 1
    )
    for block in range(blocks):
        row = block * BLOCK
        first = coupling(row) + jnp.where(diagonal, keep_ref[pl.ds(row, 1), :], 0.0)
        map_ref[block, pl.ds(0, width), :] = first
        map_ref[block, pl.ds(width, PAD), :] = jnp.broadcast_to(
            offset_ref[pl.ds(row, 1), :], (PAD, width)
        )
        acc_ref[block] = first * cotan_ref[pl.ds(row, 1), :]

    def gather_step(step, carry):
        for block in range(blocks):
            row = block * BLOCK + step
            mapped = map_ref[block]
            moved = mapped * keep_ref[pl.ds(row, 1), :] + product(mapped, coupling(row))
            map_ref[block, pl.ds(0, width), :] = moved[:width]
            map_ref[block, pl.ds(width, PAD), :] = moved[width:] + offset_ref[pl.ds(row, 1), :]
            acc_ref[block] += moved[:width] * cotan_ref[pl.ds(row, 1), :]
        return carry

    lax.fori_loop(1, BLOCK, gather_step, 0)

    levels = [[(map_ref[block], row_sums(acc_ref[block])) for block in range(blocks)]]
    while len(levels[-1]) > 1:
        nodes = levels[-1]
        levels.append([merge(nodes[i], nodes[i + 1]) for i in range(0, len(nodes), 2)])

    node = levels[-1][0]
    tall = width + PAD
    copies = []
    for level in range(len(GROUP_LEVELS)):
        side = sides[level]
        pair_ref[level, side, pl.ds(0, tall), :] = node[0]
        pair_ref[level, side, pl.ds(tall, PAD), :] = node[1]
        copy = pltpu.make_async_remote_copy(
            src_ref=pair_ref.at[level, side],
            dst_ref=pair_ref.at[level, side],
            send_sem=pair_send.at[level],
            recv_sem=pair_recv.at[level],
            device_id=at(partners[level]),
        )
        copy.start()
        copies.append(copy)
        copy.wait_recv()
        node = merge(
            *[
                (pair_ref[level, i, pl.ds(0, tall), :], pair_ref[level, i, pl.ds(tall, PAD), :])
                for i in (0, 1)
            ]
        )

    ahead_copy = pltpu.make_async_remote_copy(
        src_ref=out_ahead_ref,
        dst_ref=ahead_ref,
        send_sem=ahead_sems.at[0],
        recv_sem=ahead_sems.at[1],
        device_id=at(me + GROUP),
    )
    behind_copy = pltpu.make_async_remote_copy(
        src_ref=out_behind_ref,
        dst_ref=behind_ref,
        send_sem=behind_sems.at[0],
        recv_sem=behind_sems.at[1],
        device_id=at(me - GROUP),
    )

    def pass_forward():
        @pl.when(group == 0)
        def _():
            ahead_ref[...] = jnp.broadcast_to(initial_ref[...], ahead_ref.shape)

        @pl.when(group > 0)
        def _():
            ahead_copy.wait_recv()

        @pl.when(group < groups - 1)
        def _():
            out_ahead_ref[...] = go_forward(node, ahead_ref[...])
            ahead_copy.start()

    def pass_back():
        @pl.when(group == groups - 1)
        def _():
            behind_ref[...] = jnp.zeros_like(behind_ref)

        @pl.when(group < groups - 1)
        def _():
            behind_copy.wait_recv()

        @pl.when(group > 0)
        def _():
            out_behind_ref[...] = go_back(node, behind_ref[...])
            behind_copy.start()

    @pl.when(group < groups // 2)
    def _():
        pass_forward()
        pass_back()

    @pl.when(group >= groups // 2)
    def _():
        pass_back()
        pass_forward()

    state = ahead_ref[...]
    costate = behind_ref[...]
    for level in reversed(range(len(GROUP_LEVELS))):
        early, late = [
            (pair_ref[level, i, pl.ds(0, tall), :], pair_ref[level, i, pl.ds(tall, PAD), :])
            for i in (0, 1)
        ]
        is_late = sides[level] == 1
        state, costate = (
            jnp.where(is_late, go_forward(early, state), state),
            jnp.where(is_late, costate, go_back(late, costate)),
        )

    entries = [(state, costate)]
    for nodes in reversed(levels[:-1]):
        finer = []
        for i, (state, costate) in enumerate(entries):
            early, late = nodes[2 * i], nodes[2 * i + 1]
            finer.append((state, go_back(late, costate)))
            finer.append((go_forward(early, state), costate))
        entries = finer

    states = jnp.concatenate([entry[0][:1] for entry in entries], axis=0)
    costates = jnp.concatenate([entry[1][:1] for entry in entries], axis=0)
    weight_high, weight_low = split(weight_ref[...])

    def apply_step(step, carry):
        states, costates = carry
        now = pl.ds(step, blocks, stride=BLOCK)
        mapped = few_rows(states, weight_high, weight_low, NN)
        states = keep_ref[now, :] * states + offset_ref[now, :]
        for part in range(3):
            columns = slice(part * width, (part + 1) * width)
            states = states + term_ref[part, now, :] * mapped[:, columns]
        state_out[now, :] = states

        back = pl.ds(BLOCK - 1 - step, blocks, stride=BLOCK)
        costates = cotan_ref[back, :] + costates
        adjoint_out[back, :] = costates
        spread = jnp.concatenate(
            [term_ref[part, back, :] * costates for part in range(3)], axis=1
        )
        costates = keep_ref[back, :] * costates + few_rows(spread, weight_high, weight_low, NT)
        return states, costates

    lax.fori_loop(0, BLOCK, apply_step, (states, costates))

    @pl.when(me < seq_count - 1)
    def _():
        row_copy.wait_send()

    for copy in copies:
        copy.wait_send()

    @pl.when(group < groups - 1)
    def _():
        ahead_copy.wait_send()

    @pl.when(group > 0)
    def _():
        behind_copy.wait_send()


def per_device(
    seq_count, inputs, trajectory, initial_state, cotangent, in_weight, recurrent_weight, gate_bias
):
    rows, width = trajectory.shape[1:]
    blocks = rows // BLOCK
    out = jax.ShapeDtypeStruct((rows, width), jnp.float32)
    tall = width + PAD
    vmem = functools.partial(pltpu.VMEM, dtype=jnp.float32)
    pair_sems = pltpu.SemaphoreType.DMA((2,))
    new_state, adjoint = pl.pallas_call(
        functools.partial(kernel, seq_count),
        out_shape=(out, out),
        in_specs=[pl.BlockSpec(memory_space=pltpu.VMEM)] * 7,
        out_specs=(pl.BlockSpec(memory_space=pltpu.VMEM),) * 2,
        scratch_shapes=[
            vmem((rows, width)),
            vmem((rows, width)),
            vmem((3, rows, width)),
            vmem((rows, width)),
            vmem((blocks, tall, width)),
            vmem((blocks, width, width)),
            vmem((len(GROUP_LEVELS), 2, tall + PAD, width)),
            vmem((8, width)),
            vmem((PAD, width)),
            vmem((PAD, width)),
            vmem((PAD, width)),
            vmem((PAD, width)),
            pair_sems,
            pltpu.SemaphoreType.DMA((len(GROUP_LEVELS),)),
            pltpu.SemaphoreType.DMA((len(GROUP_LEVELS),)),
            pair_sems,
            pair_sems,
        ],
        compiler_params=pltpu.CompilerParams(
            collective_id=0, has_side_effects=True, vmem_limit_bytes=40 * 1024 * 1024
        ),
        name="newton_step",
    )(
        inputs[0],
        trajectory[0],
        initial_state,
        cotangent[0],
        in_weight,
        recurrent_weight,
        gate_bias[None],
    )
    return new_state[None], adjoint[None]


def solution(mesh):
    return jax.shard_map(
        functools.partial(per_device, mesh.shape["seq"]),
        mesh=mesh,
        in_specs=(
            P("dp", "seq", None),
            P("dp", "seq", None),
            P("dp", None),
            P("dp", "seq", None),
            P(),
            P(),
            P(),
        ),
        out_specs=(P("dp", "seq", None), P("dp", "seq", None)),
        check_vma=False,
    )
```

```python
import functools

import jax
import jax.numpy as jnp
from jax import lax
from jax.experimental import pallas as pl
from jax.experimental.pallas import tpu as pltpu
from jax.sharding import PartitionSpec as P

BLOCK = 8
GROUP_LEVELS = (1, 2)
GROUP = 4
PAD = 16

HIGHEST_PRECISION = lax.Precision.HIGHEST
NT = (((1,), (1,)), ((), ()))
NN = (((1,), (0,)), ((), ()))


def split(value):
    high = value.astype(jnp.bfloat16)
    low = (value - high.astype(jnp.float32)).astype(jnp.bfloat16)
    return high, low


def product(rows, weights):
    high, low = split(rows)
    w_high, w_low = split(weights)
    width = weights.shape[1]
    stacked = jnp.concatenate(
        [
            jnp.concatenate([w_high, w_low], axis=1),
            jnp.concatenate([w_high, jnp.zeros_like(w_low)], axis=1),
        ],
        axis=0,
    )
    out = jnp.dot(
        jnp.concatenate([high, low], axis=1), stacked, preferred_element_type=jnp.float32
    )
    return out[:, :width] + out[:, width:]


def few_rows(rows, w_high, w_low, dims):
    high, low = split(rows)
    count = rows.shape[0]
    both = lax.dot_general(
        jnp.concatenate([high, low], axis=0), w_high, dims, preferred_element_type=jnp.float32
    )
    extra = lax.dot_general(high, w_low, dims, preferred_element_type=jnp.float32)
    return both[:count] + both[count:] + extra


def row_sums(matrix):
    high, low = split(matrix)
    ones = jnp.ones((PAD, matrix.shape[1]), jnp.bfloat16)
    total = lax.dot_general(ones, high, NT, preferred_element_type=jnp.float32)
    return total + lax.dot_general(ones, low, NT, preferred_element_type=jnp.float32)


def merge(early, late):
    early_map, early_adjoint = early
    late_map, late_adjoint = late
    width = early_map.shape[1]
    merged = product(early_map, late_map[:width])
    merged = jnp.concatenate([merged[:width], merged[width:] + late_map[width:]], axis=0)
    high, low = split(early_map[:width])
    adjoint = early_adjoint + few_rows(late_adjoint, high, low, NT)
    return merged, adjoint


def in_parts(node):
    mapped, adjoint = node
    width = mapped.shape[1]
    return (*split(mapped[:width]), mapped[width:], adjoint)


def go_forward(parts, state):
    high, low, offset, _ = parts
    return few_rows(state, high, low, NN) + offset


def go_back(parts, costate):
    high, low, _, adjoint = parts
    return few_rows(costate, high, low, NT) + adjoint


def kernel(
    seq_count,
    features_hbm,
    path_hbm,
    initial_hbm,
    cotan_hbm,
    in_weight_hbm,
    weight_hbm,
    bias_hbm,
    state_out,
    adjoint_out,
    features_ref,
    path_ref,
    initial_ref,
    cotan_ref,
    in_weight_ref,
    weight_ref,
    bias_ref,
    fetch_sems,
    previous_ref,
    keep_ref,
    term_ref,
    offset_ref,
    map_ref,
    acc_ref,
    pair_ref,
    row_ref,
    ahead_ref,
    behind_ref,
    out_ahead_ref,
    out_behind_ref,
    row_sems,
    pair_send,
    pair_recv,
    ahead_sems,
    behind_sems,
):
    rows, width = path_hbm.shape
    blocks = rows // BLOCK
    me = lax.axis_index("seq")
    groups = seq_count // GROUP
    group = me // GROUP

    def at(place):
        return {"seq": place}

    fetches = []
    for source, target in (
        (path_hbm, path_ref),
        (features_hbm, features_ref),
        (in_weight_hbm, in_weight_ref),
        (bias_hbm, bias_ref),
        (weight_hbm, weight_ref),
        (initial_hbm, initial_ref),
        (cotan_hbm, cotan_ref),
    ):
        fetch = pltpu.make_async_copy(source, target, fetch_sems.at[len(fetches)])
        fetch.start()
        fetches.append(fetch)

    barrier = pltpu.get_barrier_semaphore()
    greeted = jnp.int32(0)
    for distance in (1, GROUP):

        @pl.when(me >= distance)
        def _():
            pl.semaphore_signal(barrier, inc=1, device_id=at(me - distance))

        @pl.when(me < seq_count - distance)
        def _():
            pl.semaphore_signal(barrier, inc=1, device_id=at(me + distance))

        greeted = greeted + jnp.where(me >= distance, 1, 0)
        greeted = greeted + jnp.where(me < seq_count - distance, 1, 0)
    sides = [(me // bit) % 2 for bit in GROUP_LEVELS]
    partners = [me + bit - 2 * bit * side for bit, side in zip(GROUP_LEVELS, sides)]
    for partner in partners[1:]:
        pl.semaphore_signal(barrier, inc=1, device_id=at(partner))
        greeted = greeted + 1
    pl.semaphore_wait(barrier, greeted)

    row_copy = pltpu.make_async_remote_copy(
        src_ref=path_hbm.at[pl.ds(rows - 8, 8)],
        dst_ref=row_ref,
        send_sem=row_sems.at[0],
        recv_sem=row_sems.at[1],
        device_id=at(me + 1),
    )

    @pl.when(me < seq_count - 1)
    def _():
        row_copy.start()

    for fetch in fetches[:4]:
        fetch.wait()

    projected = (
        jnp.dot(
            features_ref[...],
            in_weight_ref[...],
            precision=HIGHEST_PRECISION,
            preferred_element_type=jnp.float32,
        )
        + bias_ref[...][None, :]
    )
    previous_ref[pl.ds(1, rows - 1), :] = path_ref[pl.ds(0, rows - 1), :]

    for fetch in fetches[4:]:
        fetch.wait()

    @pl.when(me > 0)
    def _():
        row_copy.wait_recv()
        previous_ref[pl.ds(0, 1), :] = row_ref[pl.ds(7, 1), :]

    @pl.when(me == 0)
    def _():
        previous_ref[pl.ds(0, 1), :] = initial_ref[...]

    previous = previous_ref[...]
    recurrent = jnp.dot(
        previous,
        weight_ref[...],
        precision=HIGHEST_PRECISION,
        preferred_element_type=jnp.float32,
    )
    reset_gate = jax.nn.sigmoid(projected[:, :width] + recurrent[:, :width])
    write_gate = jax.nn.sigmoid(
        projected[:, width : 2 * width] + recurrent[:, width : 2 * width]
    )
    cand_recurrent = recurrent[:, 2 * width :]
    candidate = jnp.tanh(projected[:, 2 * width :] + reset_gate * cand_recurrent)
    updated = previous + write_gate * (candidate - previous)
    keep_rate = 1.0 - write_gate
    slopes = write_gate * (1.0 - candidate * candidate)
    reset_terms = slopes * cand_recurrent * reset_gate * (1.0 - reset_gate)
    write_terms = (candidate - previous) * write_gate * (1.0 - write_gate)
    cand_terms = slopes * reset_gate
    keep_ref[...] = keep_rate
    term_ref[0] = reset_terms
    term_ref[1] = write_terms
    term_ref[2] = cand_terms
    offset_ref[...] = (
        updated
        - keep_rate * previous
        - reset_terms * recurrent[:, :width]
        - write_terms * recurrent[:, width : 2 * width]
        - cand_terms * cand_recurrent
    )

    def coupling(row):
        total = weight_ref[:, pl.ds(0, width)] * term_ref[0, pl.ds(row, 1), :]
        for part in (1, 2):
            columns = pl.ds(part * width, width)
            total = total + weight_ref[:, columns] * term_ref[part, pl.ds(row, 1), :]
        return total

    diagonal = lax.broadcasted_iota(jnp.int32, (width, width), 0) == lax.broadcasted_iota(
        jnp.int32, (width, width), 1
    )
    for block in range(blocks):
        row = block * BLOCK
        first = coupling(row) + jnp.where(diagonal, keep_ref[pl.ds(row, 1), :], 0.0)
        map_ref[block, pl.ds(0, width), :] = first
        map_ref[block, pl.ds(width, PAD), :] = jnp.broadcast_to(
            offset_ref[pl.ds(row, 1), :], (PAD, width)
        )
        acc_ref[block] = first * cotan_ref[pl.ds(row, 1), :]

    def gather_step(step, carry):
        for block in range(blocks):
            row = block * BLOCK + step
            mapped = map_ref[block]
            moved = mapped * keep_ref[pl.ds(row, 1), :] + product(mapped, coupling(row))
            map_ref[block, pl.ds(0, width), :] = moved[:width]
            map_ref[block, pl.ds(width, PAD), :] = moved[width:] + offset_ref[pl.ds(row, 1), :]
            acc_ref[block] += moved[:width] * cotan_ref[pl.ds(row, 1), :]
        return carry

    lax.fori_loop(1, BLOCK, gather_step, 0)

    levels = [[(map_ref[block], row_sums(acc_ref[block])) for block in range(blocks)]]
    while len(levels[-1]) > 1:
        nodes = levels[-1]
        levels.append([merge(nodes[i], nodes[i + 1]) for i in range(0, len(nodes), 2)])

    node = levels[-1][0]
    tall = width + PAD
    copies = []
    pair_parts = []
    for level in range(len(GROUP_LEVELS)):
        side = sides[level]
        pair_ref[level, side, pl.ds(0, tall), :] = node[0]
        pair_ref[level, side, pl.ds(tall, PAD), :] = node[1]
        copy = pltpu.make_async_remote_copy(
            src_ref=pair_ref.at[level, side],
            dst_ref=pair_ref.at[level, side],
            send_sem=pair_send.at[level],
            recv_sem=pair_recv.at[level],
            device_id=at(partners[level]),
        )
        copy.start()
        copies.append(copy)
        copy.wait_recv()
        pair = [
            (pair_ref[level, i, pl.ds(0, tall), :], pair_ref[level, i, pl.ds(tall, PAD), :])
            for i in (0, 1)
        ]
        pair_parts.append([in_parts(one) for one in pair])
        node = merge(*pair)

    whole = in_parts(node)
    ahead_copy = pltpu.make_async_remote_copy(
        src_ref=out_ahead_ref,
        dst_ref=ahead_ref,
        send_sem=ahead_sems.at[0],
        recv_sem=ahead_sems.at[1],
        device_id=at(me + GROUP),
    )
    behind_copy = pltpu.make_async_remote_copy(
        src_ref=out_behind_ref,
        dst_ref=behind_ref,
        send_sem=behind_sems.at[0],
        recv_sem=behind_sems.at[1],
        device_id=at(me - GROUP),
    )

    def pass_forward():
        @pl.when(group == 0)
        def _():
            ahead_ref[...] = jnp.broadcast_to(initial_ref[...], ahead_ref.shape)

        @pl.when(group > 0)
        def _():
            ahead_copy.wait_recv()

        @pl.when(group < groups - 1)
        def _():
            out_ahead_ref[...] = go_forward(whole, ahead_ref[...])
            ahead_copy.start()

    def pass_back():
        @pl.when(group == groups - 1)
        def _():
            behind_ref[...] = jnp.zeros_like(behind_ref)

        @pl.when(group < groups - 1)
        def _():
            behind_copy.wait_recv()

        @pl.when(group > 0)
        def _():
            out_behind_ref[...] = go_back(whole, behind_ref[...])
            behind_copy.start()

    @pl.when(group < groups // 2)
    def _():
        pass_forward()
        pass_back()

    @pl.when(group >= groups // 2)
    def _():
        pass_back()
        pass_forward()

    state = ahead_ref[...]
    costate = behind_ref[...]
    for level in reversed(range(len(GROUP_LEVELS))):
        early, late = pair_parts[level]
        is_late = sides[level] == 1
        state, costate = (
            jnp.where(is_late, go_forward(early, state), state),
            jnp.where(is_late, costate, go_back(late, costate)),
        )

    entries = [(state, costate)]
    for nodes in reversed(levels[:-1]):
        finer = []
        for i, (state, costate) in enumerate(entries):
            early, late = in_parts(nodes[2 * i]), in_parts(nodes[2 * i + 1])
            finer.append((state, go_back(late, costate)))
            finer.append((go_forward(early, state), costate))
        entries = finer

    states = jnp.concatenate([entry[0][:1] for entry in entries], axis=0)
    costates = jnp.concatenate([entry[1][:1] for entry in entries], axis=0)
    weight_high, weight_low = split(weight_ref[...])

    def apply_step(step, carry):
        states, costates = carry
        now = pl.ds(step, blocks, stride=BLOCK)
        mapped = few_rows(states, weight_high, weight_low, NN)
        states = keep_ref[now, :] * states + offset_ref[now, :]
        for part in range(3):
            columns = slice(part * width, (part + 1) * width)
            states = states + term_ref[part, now, :] * mapped[:, columns]
        state_out[now, :] = states

        back = pl.ds(BLOCK - 1 - step, blocks, stride=BLOCK)
        costates = cotan_ref[back, :] + costates
        adjoint_out[back, :] = costates
        spread = jnp.concatenate(
            [term_ref[part, back, :] * costates for part in range(3)], axis=1
        )
        costates = keep_ref[back, :] * costates + few_rows(spread, weight_high, weight_low, NT)
        return states, costates

    lax.fori_loop(0, BLOCK, apply_step, (states, costates))

    @pl.when(me < seq_count - 1)
    def _():
        row_copy.wait_send()

    for copy in copies:
        copy.wait_send()

    @pl.when(group < groups - 1)
    def _():
        ahead_copy.wait_send()

    @pl.when(group > 0)
    def _():
        behind_copy.wait_send()


def per_device(
    seq_count, inputs, trajectory, initial_state, cotangent, in_weight, recurrent_weight, gate_bias
):
    rows, width = trajectory.shape[1:]
    blocks = rows // BLOCK
    out = jax.ShapeDtypeStruct((rows, width), jnp.float32)
    tall = width + PAD
    vmem = functools.partial(pltpu.VMEM, dtype=jnp.float32)
    pair_sems = pltpu.SemaphoreType.DMA((2,))
    new_state, adjoint = pl.pallas_call(
        functools.partial(kernel, seq_count),
        out_shape=(out, out),
        in_specs=[pl.BlockSpec(memory_space=pltpu.HBM)] * 7,
        out_specs=(pl.BlockSpec(memory_space=pltpu.VMEM),) * 2,
        scratch_shapes=[
            vmem(inputs.shape[1:]),
            vmem((rows, width)),
            vmem((1, width)),
            vmem((rows, width)),
            vmem(in_weight.shape),
            vmem(recurrent_weight.shape),
            vmem((3 * width,)),
            pltpu.SemaphoreType.DMA((7,)),
            vmem((rows, width)),
            vmem((rows, width)),
            vmem((3, rows, width)),
            vmem((rows, width)),
            vmem((blocks, tall, width)),
            vmem((blocks, width, width)),
            vmem((len(GROUP_LEVELS), 2, tall + PAD, width)),
            vmem((8, width)),
            vmem((PAD, width)),
            vmem((PAD, width)),
            vmem((PAD, width)),
            vmem((PAD, width)),
            pair_sems,
            pltpu.SemaphoreType.DMA((len(GROUP_LEVELS),)),
            pltpu.SemaphoreType.DMA((len(GROUP_LEVELS),)),
            pair_sems,
            pair_sems,
        ],
        compiler_params=pltpu.CompilerParams(
            collective_id=0, has_side_effects=True, vmem_limit_bytes=64 * 1024 * 1024
        ),
        name="newton_step",
    )(
        inputs[0],
        trajectory[0],
        initial_state,
        cotangent[0],
        in_weight,
        recurrent_weight,
        gate_bias,
    )
    return new_state[None], adjoint[None]


def solution(mesh):
    return jax.shard_map(
        functools.partial(per_device, mesh.shape["seq"]),
        mesh=mesh,
        in_specs=(
            P("dp", "seq", None),
            P("dp", "seq", None),
            P("dp", None),
            P("dp", "seq", None),
            P(),
            P(),
            P(),
        ),
        out_specs=(P("dp", "seq", None), P("dp", "seq", None)),
        check_vma=False,
    )
```

```python
import functools

import jax
import jax.numpy as jnp
from jax import lax
from jax.experimental import pallas as pl
from jax.experimental.pallas import tpu as pltpu
from jax.sharding import PartitionSpec as P

BLOCK = 8
GROUP_LEVELS = (1, 2)
GROUP = 4
PAD = 16

NT = (((1,), (1,)), ((), ()))
NN = (((1,), (0,)), ((), ()))


def split(value):
    high = value.astype(jnp.bfloat16)
    low = (value - high.astype(jnp.float32)).astype(jnp.bfloat16)
    return high, low


def product_of_parts(rows, weights):
    (high, low), (w_high, w_low) = rows, weights
    width = w_high.shape[1]
    stacked = jnp.concatenate(
        [
            jnp.concatenate([w_high, w_low], axis=1),
            jnp.concatenate([w_high, jnp.zeros_like(w_low)], axis=1),
        ],
        axis=0,
    )
    out = jnp.dot(
        jnp.concatenate([high, low], axis=1), stacked, preferred_element_type=jnp.float32
    )
    return out[:, :width] + out[:, width:]


def product(rows, weights):
    return product_of_parts(split(rows), split(weights))


def few_rows(rows, parts, dims):
    count = rows.shape[0]
    side = 1 - dims[0][1][0]
    width = parts[0].shape[side]
    out = lax.dot_general(
        jnp.concatenate(split(rows), axis=0),
        jnp.concatenate(parts, axis=side),
        dims,
        preferred_element_type=jnp.float32,
    )
    return out[:count, :width] + out[count:, :width] + out[:count, width:]


def row_sums(matrix):
    ones = jnp.ones((PAD, 2 * matrix.shape[1]), jnp.bfloat16)
    return lax.dot_general(
        ones,
        jnp.concatenate(split(matrix), axis=1),
        NT,
        preferred_element_type=jnp.float32,
    )


def node_of(mapped, adjoint):
    return mapped, split(mapped), adjoint


def matrix_parts(node):
    width = node[0].shape[1]
    return tuple(part[:width] for part in node[1])


def merge(early, late):
    width = early[0].shape[1]
    merged = product_of_parts(early[1], matrix_parts(late))
    merged = jnp.concatenate([merged[:width], merged[width:] + late[0][width:]], axis=0)
    return node_of(merged, early[2] + few_rows(late[2], matrix_parts(early), NT))


def go_forward(node, state):
    return few_rows(state, matrix_parts(node), NN) + node[0][state.shape[1] :]


def go_back(node, costate):
    return few_rows(costate, matrix_parts(node), NT) + node[2]


def kernel(
    seq_count,
    features_hbm,
    path_hbm,
    initial_hbm,
    cotan_hbm,
    in_weight_hbm,
    weight_hbm,
    bias_hbm,
    state_out,
    adjoint_out,
    features_ref,
    path_ref,
    initial_ref,
    cotan_ref,
    in_weight_ref,
    weight_ref,
    bias_ref,
    fetch_sems,
    previous_ref,
    keep_ref,
    term_ref,
    offset_ref,
    map_ref,
    acc_ref,
    pair_ref,
    row_ref,
    ahead_ref,
    behind_ref,
    out_ahead_ref,
    out_behind_ref,
    row_sems,
    pair_send,
    pair_recv,
    ahead_sems,
    behind_sems,
):
    rows, width = path_hbm.shape
    blocks = rows // BLOCK
    me = lax.axis_index("seq")
    groups = seq_count // GROUP
    group = me // GROUP

    def at(place):
        return {"seq": place}

    fetches = []
    for source, target in (
        (path_hbm, path_ref),
        (features_hbm, features_ref),
        (in_weight_hbm, in_weight_ref),
        (bias_hbm, bias_ref),
        (weight_hbm, weight_ref),
        (initial_hbm, initial_ref),
        (cotan_hbm, cotan_ref),
    ):
        fetch = pltpu.make_async_copy(source, target, fetch_sems.at[len(fetches)])
        fetch.start()
        fetches.append(fetch)

    barrier = pltpu.get_barrier_semaphore()
    greeted = jnp.int32(0)
    for distance in (1, GROUP):

        @pl.when(me >= distance)
        def _():
            pl.semaphore_signal(barrier, inc=1, device_id=at(me - distance))

        @pl.when(me < seq_count - distance)
        def _():
            pl.semaphore_signal(barrier, inc=1, device_id=at(me + distance))

        greeted = greeted + jnp.where(me >= distance, 1, 0)
        greeted = greeted + jnp.where(me < seq_count - distance, 1, 0)
    sides = [(me // bit) % 2 for bit in GROUP_LEVELS]
    partners = [me + bit - 2 * bit * side for bit, side in zip(GROUP_LEVELS, sides)]
    for partner in partners[1:]:
        pl.semaphore_signal(barrier, inc=1, device_id=at(partner))
        greeted = greeted + 1
    pl.semaphore_wait(barrier, greeted)

    row_copy = pltpu.make_async_remote_copy(
        src_ref=path_hbm.at[pl.ds(rows - 8, 8)],
        dst_ref=row_ref,
        send_sem=row_sems.at[0],
        recv_sem=row_sems.at[1],
        device_id=at(me + 1),
    )

    @pl.when(me < seq_count - 1)
    def _():
        row_copy.start()

    for fetch in fetches[:4]:
        fetch.wait()

    projected = (
        product(features_ref[...], in_weight_ref[...])
        + bias_ref[...][None, :]
    )
    previous_ref[pl.ds(1, rows - 1), :] = path_ref[pl.ds(0, rows - 1), :]

    for fetch in fetches[4:]:
        fetch.wait()

    @pl.when(me > 0)
    def _():
        row_copy.wait_recv()
        previous_ref[pl.ds(0, 1), :] = row_ref[pl.ds(7, 1), :]

    @pl.when(me == 0)
    def _():
        previous_ref[pl.ds(0, 1), :] = initial_ref[...]

    previous = previous_ref[...]
    weight_parts = split(weight_ref[...])
    recurrent = product_of_parts(split(previous), weight_parts)
    reset_gate = jax.nn.sigmoid(projected[:, :width] + recurrent[:, :width])
    write_gate = jax.nn.sigmoid(
        projected[:, width : 2 * width] + recurrent[:, width : 2 * width]
    )
    cand_recurrent = recurrent[:, 2 * width :]
    candidate = jnp.tanh(projected[:, 2 * width :] + reset_gate * cand_recurrent)
    updated = previous + write_gate * (candidate - previous)
    keep_rate = 1.0 - write_gate
    slopes = write_gate * (1.0 - candidate * candidate)
    reset_terms = slopes * cand_recurrent * reset_gate * (1.0 - reset_gate)
    write_terms = (candidate - previous) * write_gate * (1.0 - write_gate)
    cand_terms = slopes * reset_gate
    keep_ref[...] = keep_rate
    term_ref[0] = reset_terms
    term_ref[1] = write_terms
    term_ref[2] = cand_terms
    offset_ref[...] = (
        updated
        - keep_rate * previous
        - reset_terms * recurrent[:, :width]
        - write_terms * recurrent[:, width : 2 * width]
        - cand_terms * cand_recurrent
    )

    def coupling(row):
        total = weight_ref[:, pl.ds(0, width)] * term_ref[0, pl.ds(row, 1), :]
        for part in (1, 2):
            columns = pl.ds(part * width, width)
            total = total + weight_ref[:, columns] * term_ref[part, pl.ds(row, 1), :]
        return total

    diagonal = lax.broadcasted_iota(jnp.int32, (width, width), 0) == lax.broadcasted_iota(
        jnp.int32, (width, width), 1
    )
    for block in range(blocks):
        row = block * BLOCK
        first = coupling(row) + jnp.where(diagonal, keep_ref[pl.ds(row, 1), :], 0.0)
        map_ref[block, pl.ds(0, width), :] = first
        map_ref[block, pl.ds(width, PAD), :] = jnp.broadcast_to(
            offset_ref[pl.ds(row, 1), :], (PAD, width)
        )
        acc_ref[block] = first * cotan_ref[pl.ds(row, 1), :]

    def gather_step(step, carry):
        for block in range(blocks):
            row = block * BLOCK + step
            mapped = map_ref[block]
            moved = mapped * keep_ref[pl.ds(row, 1), :] + product(mapped, coupling(row))
            map_ref[block, pl.ds(0, width), :] = moved[:width]
            map_ref[block, pl.ds(width, PAD), :] = moved[width:] + offset_ref[pl.ds(row, 1), :]
            acc_ref[block] += moved[:width] * cotan_ref[pl.ds(row, 1), :]
        return carry

    lax.fori_loop(1, BLOCK, gather_step, 0)

    levels = [[node_of(map_ref[block], row_sums(acc_ref[block])) for block in range(blocks)]]
    while len(levels[-1]) > 1:
        nodes = levels[-1]
        levels.append([merge(nodes[i], nodes[i + 1]) for i in range(0, len(nodes), 2)])

    node = levels[-1][0]
    tall = width + PAD
    copies = []
    pairs = []
    for level in range(len(GROUP_LEVELS)):
        side = sides[level]
        pair_ref[level, side, pl.ds(0, tall), :] = node[0]
        pair_ref[level, side, pl.ds(tall, PAD), :] = node[2]
        copy = pltpu.make_async_remote_copy(
            src_ref=pair_ref.at[level, side],
            dst_ref=pair_ref.at[level, side],
            send_sem=pair_send.at[level],
            recv_sem=pair_recv.at[level],
            device_id=at(partners[level]),
        )
        copy.start()
        copies.append(copy)
        copy.wait_recv()
        pair = [
            node_of(pair_ref[level, i, pl.ds(0, tall), :], pair_ref[level, i, pl.ds(tall, PAD), :])
            for i in (0, 1)
        ]
        pairs.append(pair)
        node = merge(*pair)

    ahead_copy = pltpu.make_async_remote_copy(
        src_ref=out_ahead_ref,
        dst_ref=ahead_ref,
        send_sem=ahead_sems.at[0],
        recv_sem=ahead_sems.at[1],
        device_id=at(me + GROUP),
    )
    behind_copy = pltpu.make_async_remote_copy(
        src_ref=out_behind_ref,
        dst_ref=behind_ref,
        send_sem=behind_sems.at[0],
        recv_sem=behind_sems.at[1],
        device_id=at(me - GROUP),
    )

    def pass_forward():
        @pl.when(group == 0)
        def _():
            ahead_ref[...] = jnp.broadcast_to(initial_ref[...], ahead_ref.shape)

        @pl.when(group > 0)
        def _():
            ahead_copy.wait_recv()

        @pl.when(group < groups - 1)
        def _():
            out_ahead_ref[...] = go_forward(node, ahead_ref[...])
            ahead_copy.start()

    def pass_back():
        @pl.when(group == groups - 1)
        def _():
            behind_ref[...] = jnp.zeros_like(behind_ref)

        @pl.when(group < groups - 1)
        def _():
            behind_copy.wait_recv()

        @pl.when(group > 0)
        def _():
            out_behind_ref[...] = go_back(node, behind_ref[...])
            behind_copy.start()

    @pl.when(group < groups // 2)
    def _():
        pass_forward()
        pass_back()

    @pl.when(group >= groups // 2)
    def _():
        pass_back()
        pass_forward()

    state = ahead_ref[...]
    costate = behind_ref[...]
    for level in reversed(range(len(GROUP_LEVELS))):
        early, late = pairs[level]
        is_late = sides[level] == 1
        state, costate = (
            jnp.where(is_late, go_forward(early, state), state),
            jnp.where(is_late, costate, go_back(late, costate)),
        )

    entries = [(state, costate)]
    for nodes in reversed(levels[:-1]):
        finer = []
        for i, (state, costate) in enumerate(entries):
            early, late = nodes[2 * i], nodes[2 * i + 1]
            finer.append((state, go_back(late, costate)))
            finer.append((go_forward(early, state), costate))
        entries = finer

    states = jnp.concatenate([entry[0][:1] for entry in entries], axis=0)
    costates = jnp.concatenate([entry[1][:1] for entry in entries], axis=0)

    def apply_step(step, carry):
        states, costates = carry
        now = pl.ds(step, blocks, stride=BLOCK)
        mapped = few_rows(states, weight_parts, NN)
        states = keep_ref[now, :] * states + offset_ref[now, :]
        for part in range(3):
            columns = slice(part * width, (part + 1) * width)
            states = states + term_ref[part, now, :] * mapped[:, columns]
        state_out[now, :] = states

        back = pl.ds(BLOCK - 1 - step, blocks, stride=BLOCK)
        costates = cotan_ref[back, :] + costates
        adjoint_out[back, :] = costates
        spread = jnp.concatenate(
            [term_ref[part, back, :] * costates for part in range(3)], axis=1
        )
        costates = keep_ref[back, :] * costates + few_rows(spread, weight_parts, NT)
        return states, costates

    lax.fori_loop(0, BLOCK, apply_step, (states, costates))

    @pl.when(me < seq_count - 1)
    def _():
        row_copy.wait_send()

    for copy in copies:
        copy.wait_send()

    @pl.when(group < groups - 1)
    def _():
        ahead_copy.wait_send()

    @pl.when(group > 0)
    def _():
        behind_copy.wait_send()


def per_device(
    seq_count, inputs, trajectory, initial_state, cotangent, in_weight, recurrent_weight, gate_bias
):
    rows, width = trajectory.shape[1:]
    blocks = rows // BLOCK
    out = jax.ShapeDtypeStruct((rows, width), jnp.float32)
    tall = width + PAD
    vmem = functools.partial(pltpu.VMEM, dtype=jnp.float32)
    pair_sems = pltpu.SemaphoreType.DMA((2,))
    new_state, adjoint = pl.pallas_call(
        functools.partial(kernel, seq_count),
        out_shape=(out, out),
        in_specs=[pl.BlockSpec(memory_space=pltpu.HBM)] * 7,
        out_specs=(pl.BlockSpec(memory_space=pltpu.VMEM),) * 2,
        scratch_shapes=[
            vmem(inputs.shape[1:]),
            vmem((rows, width)),
            vmem((1, width)),
            vmem((rows, width)),
            vmem(in_weight.shape),
            vmem(recurrent_weight.shape),
            vmem((3 * width,)),
            pltpu.SemaphoreType.DMA((7,)),
            vmem((rows, width)),
            vmem((rows, width)),
            vmem((3, rows, width)),
            vmem((rows, width)),
            vmem((blocks, tall, width)),
            vmem((blocks, width, width)),
            vmem((len(GROUP_LEVELS), 2, tall + PAD, width)),
            vmem((8, width)),
            vmem((PAD, width)),
            vmem((PAD, width)),
            vmem((PAD, width)),
            vmem((PAD, width)),
            pair_sems,
            pltpu.SemaphoreType.DMA((len(GROUP_LEVELS),)),
            pltpu.SemaphoreType.DMA((len(GROUP_LEVELS),)),
            pair_sems,
            pair_sems,
        ],
        compiler_params=pltpu.CompilerParams(
            collective_id=0, has_side_effects=True, vmem_limit_bytes=64 * 1024 * 1024
        ),
        name="newton_step",
    )(
        inputs[0],
        trajectory[0],
        initial_state,
        cotangent[0],
        in_weight,
        recurrent_weight,
        gate_bias,
    )
    return new_state[None], adjoint[None]


def solution(mesh):
    return jax.shard_map(
        functools.partial(per_device, mesh.shape["seq"]),
        mesh=mesh,
        in_specs=(
            P("dp", "seq", None),
            P("dp", "seq", None),
            P("dp", None),
            P("dp", "seq", None),
            P(),
            P(),
            P(),
        ),
        out_specs=(P("dp", "seq", None), P("dp", "seq", None)),
        check_vma=False,
    )
```

```python
import functools

import jax
import jax.numpy as jnp
from jax import lax
from jax.experimental import pallas as pl
from jax.experimental.pallas import tpu as pltpu
from jax.sharding import PartitionSpec as P

BLOCK = 8
GROUP_LEVELS = (1, 2)
GROUP = 4
PAD = 16

NT = (((1,), (1,)), ((), ()))
NN = (((1,), (0,)), ((), ()))


def split(value):
    high = value.astype(jnp.bfloat16)
    low = (value - high.astype(jnp.float32)).astype(jnp.bfloat16)
    return high, low


def product_of_parts(rows, weights):
    (high, low), (w_high, w_low) = rows, weights
    width = w_high.shape[1]
    stacked = jnp.concatenate(
        [
            jnp.concatenate([w_high, w_low], axis=1),
            jnp.concatenate([w_high, jnp.zeros_like(w_low)], axis=1),
        ],
        axis=0,
    )
    out = jnp.dot(
        jnp.concatenate([high, low], axis=1), stacked, preferred_element_type=jnp.float32
    )
    return out[:, :width] + out[:, width:]


def product(rows, weights):
    return product_of_parts(split(rows), split(weights))


def few_rows(rows, parts, dims):
    count = rows.shape[0]
    side = 1 - dims[0][1][0]
    width = parts[0].shape[side]
    out = lax.dot_general(
        jnp.concatenate(split(rows), axis=0),
        jnp.concatenate(parts, axis=side),
        dims,
        preferred_element_type=jnp.float32,
    )
    return out[:count, :width] + out[count:, :width] + out[:count, width:]


def row_sums(matrix):
    ones = jnp.ones((PAD, 2 * matrix.shape[1]), jnp.bfloat16)
    return lax.dot_general(
        ones,
        jnp.concatenate(split(matrix), axis=1),
        NT,
        preferred_element_type=jnp.float32,
    )


def node_of(mapped, adjoint):
    return mapped, split(mapped), adjoint


def matrix_parts(node):
    width = node[0].shape[1]
    return tuple(part[:width] for part in node[1])


def merge(early, late):
    width = early[0].shape[1]
    merged = product_of_parts(early[1], matrix_parts(late))
    merged = jnp.concatenate([merged[:width], merged[width:] + late[0][width:]], axis=0)
    return node_of(merged, early[2] + few_rows(late[2], matrix_parts(early), NT))


def go_forward(node, state):
    return few_rows(state, matrix_parts(node), NN) + node[0][state.shape[1] :]


def go_back(node, costate):
    return few_rows(costate, matrix_parts(node), NT) + node[2]


def kernel(
    seq_count,
    features_hbm,
    path_hbm,
    initial_hbm,
    cotan_hbm,
    in_weight_hbm,
    weight_hbm,
    bias_hbm,
    state_out,
    adjoint_out,
    features_ref,
    path_ref,
    initial_ref,
    cotan_ref,
    in_weight_ref,
    weight_ref,
    bias_ref,
    fetch_sems,
    previous_ref,
    keep_ref,
    term_ref,
    offset_ref,
    map_ref,
    acc_ref,
    pair_ref,
    row_ref,
    ahead_ref,
    behind_ref,
    out_ahead_ref,
    out_behind_ref,
    row_sems,
    pair_send,
    pair_recv,
    ahead_sems,
    behind_sems,
):
    rows, width = path_hbm.shape
    blocks = rows // BLOCK
    me = lax.axis_index("seq")
    groups = seq_count // GROUP
    group = me // GROUP

    def at(place):
        return {"seq": place}

    fetches = []
    for source, target in (
        (path_hbm, path_ref),
        (features_hbm, features_ref),
        (in_weight_hbm, in_weight_ref),
        (bias_hbm, bias_ref),
        (weight_hbm, weight_ref),
        (initial_hbm, initial_ref),
        (cotan_hbm, cotan_ref),
    ):
        fetch = pltpu.make_async_copy(source, target, fetch_sems.at[len(fetches)])
        fetch.start()
        fetches.append(fetch)

    barrier = pltpu.get_barrier_semaphore()
    greeted = jnp.int32(0)
    for distance in (1, GROUP):

        @pl.when(me >= distance)
        def _():
            pl.semaphore_signal(barrier, inc=1, device_id=at(me - distance))

        @pl.when(me < seq_count - distance)
        def _():
            pl.semaphore_signal(barrier, inc=1, device_id=at(me + distance))

        greeted = greeted + jnp.where(me >= distance, 1, 0)
        greeted = greeted + jnp.where(me < seq_count - distance, 1, 0)
    sides = [(me // bit) % 2 for bit in GROUP_LEVELS]
    partners = [me + bit - 2 * bit * side for bit, side in zip(GROUP_LEVELS, sides)]
    for partner in partners[1:]:
        pl.semaphore_signal(barrier, inc=1, device_id=at(partner))
        greeted = greeted + 1
    pl.semaphore_wait(barrier, greeted)

    row_copy = pltpu.make_async_remote_copy(
        src_ref=path_hbm.at[pl.ds(rows - 8, 8)],
        dst_ref=row_ref,
        send_sem=row_sems.at[0],
        recv_sem=row_sems.at[1],
        device_id=at(me + 1),
    )

    @pl.when(me < seq_count - 1)
    def _():
        row_copy.start()

    for fetch in fetches[:4]:
        fetch.wait()

    projected = (
        product(features_ref[...], in_weight_ref[...])
        + bias_ref[...][None, :]
    )
    previous_ref[pl.ds(1, rows - 1), :] = path_ref[pl.ds(0, rows - 1), :]

    for fetch in fetches[4:]:
        fetch.wait()

    @pl.when(me > 0)
    def _():
        row_copy.wait_recv()
        previous_ref[pl.ds(0, 1), :] = row_ref[pl.ds(7, 1), :]

    @pl.when(me == 0)
    def _():
        previous_ref[pl.ds(0, 1), :] = initial_ref[...]

    previous = previous_ref[...]
    weight_parts = split(weight_ref[...])
    recurrent = product_of_parts(split(previous), weight_parts)
    reset_gate = jax.nn.sigmoid(projected[:, :width] + recurrent[:, :width])
    write_gate = jax.nn.sigmoid(
        projected[:, width : 2 * width] + recurrent[:, width : 2 * width]
    )
    cand_recurrent = recurrent[:, 2 * width :]
    candidate = jnp.tanh(projected[:, 2 * width :] + reset_gate * cand_recurrent)
    updated = previous + write_gate * (candidate - previous)
    keep_rate = 1.0 - write_gate
    slopes = write_gate * (1.0 - candidate * candidate)
    reset_terms = slopes * cand_recurrent * reset_gate * (1.0 - reset_gate)
    write_terms = (candidate - previous) * write_gate * (1.0 - write_gate)
    cand_terms = slopes * reset_gate
    keep_ref[...] = keep_rate
    term_ref[0] = reset_terms
    term_ref[1] = write_terms
    term_ref[2] = cand_terms
    offset_ref[...] = (
        updated
        - keep_rate * previous
        - reset_terms * recurrent[:, :width]
        - write_terms * recurrent[:, width : 2 * width]
        - cand_terms * cand_recurrent
    )

    def coupling(row):
        total = weight_ref[:, pl.ds(0, width)] * term_ref[0, pl.ds(row, 1), :]
        for part in (1, 2):
            columns = pl.ds(part * width, width)
            total = total + weight_ref[:, columns] * term_ref[part, pl.ds(row, 1), :]
        return total

    diagonal = lax.broadcasted_iota(jnp.int32, (width, width), 0) == lax.broadcasted_iota(
        jnp.int32, (width, width), 1
    )
    for block in range(blocks):
        row = block * BLOCK
        first = coupling(row) + jnp.where(diagonal, keep_ref[pl.ds(row, 1), :], 0.0)
        map_ref[block, pl.ds(0, width), :] = first
        map_ref[block, pl.ds(width, PAD), :] = jnp.broadcast_to(
            offset_ref[pl.ds(row, 1), :], (PAD, width)
        )
        acc_ref[block] = first * cotan_ref[pl.ds(row, 1), :]

    def gather_step(step, carry):
        for block in range(blocks):
            row = block * BLOCK + step
            mapped = map_ref[block]
            moved = mapped * keep_ref[pl.ds(row, 1), :] + product(mapped, coupling(row))
            map_ref[block, pl.ds(0, width), :] = moved[:width]
            map_ref[block, pl.ds(width, PAD), :] = moved[width:] + offset_ref[pl.ds(row, 1), :]
            acc_ref[block] += moved[:width] * cotan_ref[pl.ds(row, 1), :]
        return carry

    lax.fori_loop(1, BLOCK, gather_step, 0)

    levels = [[node_of(map_ref[block], row_sums(acc_ref[block])) for block in range(blocks)]]
    while len(levels[-1]) > 1:
        nodes = levels[-1]
        levels.append([merge(nodes[i], nodes[i + 1]) for i in range(0, len(nodes), 2)])

    node = levels[-1][0]
    tall = width + PAD
    copies = []
    pairs = []
    for level in range(len(GROUP_LEVELS)):
        side = sides[level]
        pair_ref[level, side, pl.ds(0, tall), :] = node[0]
        pair_ref[level, side, pl.ds(tall, PAD), :] = node[2]
        copy = pltpu.make_async_remote_copy(
            src_ref=pair_ref.at[level, side],
            dst_ref=pair_ref.at[level, side],
            send_sem=pair_send.at[level],
            recv_sem=pair_recv.at[level],
            device_id=at(partners[level]),
        )
        copy.start()
        copies.append(copy)
        copy.wait_recv()
        pair = [
            node_of(pair_ref[level, i, pl.ds(0, tall), :], pair_ref[level, i, pl.ds(tall, PAD), :])
            for i in (0, 1)
        ]
        pairs.append(pair)
        node = merge(*pair)

    ahead_copy = pltpu.make_async_remote_copy(
        src_ref=out_ahead_ref,
        dst_ref=ahead_ref,
        send_sem=ahead_sems.at[0],
        recv_sem=ahead_sems.at[1],
        device_id=at(me + GROUP),
    )
    behind_copy = pltpu.make_async_remote_copy(
        src_ref=out_behind_ref,
        dst_ref=behind_ref,
        send_sem=behind_sems.at[0],
        recv_sem=behind_sems.at[1],
        device_id=at(me - GROUP),
    )

    def pass_forward():
        @pl.when(group == 0)
        def _():
            ahead_ref[...] = jnp.broadcast_to(initial_ref[...], ahead_ref.shape)

        @pl.when(group > 0)
        def _():
            ahead_copy.wait_recv()

        @pl.when(group < groups - 1)
        def _():
            out_ahead_ref[...] = go_forward(node, ahead_ref[...])
            ahead_copy.start()

    def pass_back():
        @pl.when(group == groups - 1)
        def _():
            behind_ref[...] = jnp.zeros_like(behind_ref)

        @pl.when(group < groups - 1)
        def _():
            behind_copy.wait_recv()

        @pl.when(group > 0)
        def _():
            out_behind_ref[...] = go_back(node, behind_ref[...])
            behind_copy.start()

    @pl.when(group < groups // 2)
    def _():
        pass_forward()
        pass_back()

    @pl.when(group >= groups // 2)
    def _():
        pass_back()
        pass_forward()

    state = ahead_ref[...]
    costate = behind_ref[...]
    for level in reversed(range(len(GROUP_LEVELS))):
        early, late = pairs[level]
        is_late = sides[level] == 1
        state, costate = (
            jnp.where(is_late, go_forward(early, state), state),
            jnp.where(is_late, costate, go_back(late, costate)),
        )

    entries = [(state, costate)]
    for nodes in reversed(levels[:-1]):
        finer = []
        for i, (state, costate) in enumerate(entries):
            early, late = nodes[2 * i], nodes[2 * i + 1]
            finer.append((state, go_back(late, costate)))
            finer.append((go_forward(early, state), costate))
        entries = finer

    states = jnp.concatenate([entry[0][:1] for entry in entries], axis=0)
    costates = jnp.concatenate([entry[1][:1] for entry in entries], axis=0)

    def apply_step(step, carry):
        states, costates = carry
        now = pl.ds(step, blocks, stride=BLOCK)
        mapped = few_rows(states, weight_parts, NN)
        states = keep_ref[now, :] * states + offset_ref[now, :]
        for part in range(3):
            columns = slice(part * width, (part + 1) * width)
            states = states + term_ref[part, now, :] * mapped[:, columns]
        state_out[now, :] = states

        back = pl.ds(BLOCK - 1 - step, blocks, stride=BLOCK)
        costates = cotan_ref[back, :] + costates
        adjoint_out[back, :] = costates
        spread = jnp.concatenate(
            [term_ref[part, back, :] * costates for part in range(3)], axis=1
        )
        costates = keep_ref[back, :] * costates + few_rows(spread, weight_parts, NT)
        return states, costates

    lax.fori_loop(0, BLOCK, apply_step, (states, costates))

    @pl.when(me < seq_count - 1)
    def _():
        row_copy.wait_send()

    for copy in copies:
        copy.wait_send()

    @pl.when(group < groups - 1)
    def _():
        ahead_copy.wait_send()

    @pl.when(group > 0)
    def _():
        behind_copy.wait_send()


def hand_over_kernel(state_in, adjoint_in, state_out, adjoint_out, sems):
    copies = [
        pltpu.make_async_copy(source, target, sems.at[index])
        for index, (source, target) in enumerate(
            ((state_in, state_out), (adjoint_in, adjoint_out))
        )
    ]
    for copy in copies:
        copy.start()
    for copy in copies:
        copy.wait()


def per_device(
    seq_count, inputs, trajectory, initial_state, cotangent, in_weight, recurrent_weight, gate_bias
):
    rows, width = trajectory.shape[1:]
    blocks = rows // BLOCK
    out = jax.ShapeDtypeStruct((rows, width), jnp.float32)
    tall = width + PAD
    vmem = functools.partial(pltpu.VMEM, dtype=jnp.float32)
    pair_sems = pltpu.SemaphoreType.DMA((2,))
    new_state, adjoint = pl.pallas_call(
        functools.partial(kernel, seq_count),
        out_shape=(out, out),
        in_specs=[pl.BlockSpec(memory_space=pltpu.HBM)] * 7,
        out_specs=(pl.BlockSpec(memory_space=pltpu.VMEM),) * 2,
        scratch_shapes=[
            vmem(inputs.shape[1:]),
            vmem((rows, width)),
            vmem((1, width)),
            vmem((rows, width)),
            vmem(in_weight.shape),
            vmem(recurrent_weight.shape),
            vmem((3 * width,)),
            pltpu.SemaphoreType.DMA((7,)),
            vmem((rows, width)),
            vmem((rows, width)),
            vmem((3, rows, width)),
            vmem((rows, width)),
            vmem((blocks, tall, width)),
            vmem((blocks, width, width)),
            vmem((len(GROUP_LEVELS), 2, tall + PAD, width)),
            vmem((8, width)),
            vmem((PAD, width)),
            vmem((PAD, width)),
            vmem((PAD, width)),
            vmem((PAD, width)),
            pair_sems,
            pltpu.SemaphoreType.DMA((len(GROUP_LEVELS),)),
            pltpu.SemaphoreType.DMA((len(GROUP_LEVELS),)),
            pair_sems,
            pair_sems,
        ],
        compiler_params=pltpu.CompilerParams(
            collective_id=0, has_side_effects=True, vmem_limit_bytes=64 * 1024 * 1024
        ),
        name="newton_step",
    )(
        inputs[0],
        trajectory[0],
        initial_state,
        cotangent[0],
        in_weight,
        recurrent_weight,
        gate_bias,
    )
    new_state, adjoint = pl.pallas_call(
        hand_over_kernel,
        out_shape=(out, out),
        in_specs=[pl.BlockSpec(memory_space=pl.ANY)] * 2,
        out_specs=(pl.BlockSpec(memory_space=pl.ANY),) * 2,
        scratch_shapes=[pltpu.SemaphoreType.DMA((2,))],
        compiler_params=pltpu.CompilerParams(vmem_limit_bytes=64 * 1024 * 1024),
        name="hand_over",
    )(new_state, adjoint)
    return new_state[None], adjoint[None]


def solution(mesh):
    return jax.shard_map(
        functools.partial(per_device, mesh.shape["seq"]),
        mesh=mesh,
        in_specs=(
            P("dp", "seq", None),
            P("dp", "seq", None),
            P("dp", None),
            P("dp", "seq", None),
            P(),
            P(),
            P(),
        ),
        out_specs=(P("dp", "seq", None), P("dp", "seq", None)),
        check_vma=False,
    )
```

```python
import functools

import jax
import jax.numpy as jnp
from jax import lax
from jax.experimental import pallas as pl
from jax.experimental.pallas import tpu as pltpu
from jax.sharding import PartitionSpec as P

BLOCK = 8
GROUP_LEVELS = (1, 2)
GROUP = 4
PAD = 16
SENT = 8

NT = (((1,), (1,)), ((), ()))
NN = (((1,), (0,)), ((), ()))


def split(value):
    high = value.astype(jnp.bfloat16)
    low = (value - high.astype(jnp.float32)).astype(jnp.bfloat16)
    return high, low


def product_of_parts(rows, weights):
    (high, low), (w_high, w_low) = rows, weights
    width = w_high.shape[1]
    stacked = jnp.concatenate(
        [
            jnp.concatenate([w_high, w_low], axis=1),
            jnp.concatenate([w_high, jnp.zeros_like(w_low)], axis=1),
        ],
        axis=0,
    )
    out = jnp.dot(
        jnp.concatenate([high, low], axis=1), stacked, preferred_element_type=jnp.float32
    )
    return out[:, :width] + out[:, width:]


def product(rows, weights):
    return product_of_parts(split(rows), split(weights))


def few_rows(rows, parts, dims):
    count = rows.shape[0]
    side = 1 - dims[0][1][0]
    width = parts[0].shape[side]
    out = lax.dot_general(
        jnp.concatenate(split(rows), axis=0),
        jnp.concatenate(parts, axis=side),
        dims,
        preferred_element_type=jnp.float32,
    )
    return out[:count, :width] + out[count:, :width] + out[:count, width:]


def row_sums(matrix):
    ones = jnp.ones((PAD, 2 * matrix.shape[1]), jnp.bfloat16)
    return lax.dot_general(
        ones,
        jnp.concatenate(split(matrix), axis=1),
        NT,
        preferred_element_type=jnp.float32,
    )


def node_of(mapped, adjoint):
    return mapped, split(mapped), adjoint


def matrix_parts(node):
    width = node[0].shape[1]
    return tuple(part[:width] for part in node[1])


def merge(early, late):
    width = early[0].shape[1]
    merged = product_of_parts(early[1], matrix_parts(late))
    merged = jnp.concatenate([merged[:width], merged[width:] + late[0][width:]], axis=0)
    return node_of(merged, early[2] + few_rows(late[2], matrix_parts(early), NT))


def go_forward(node, state):
    return few_rows(state, matrix_parts(node), NN) + node[0][state.shape[1] :]


def go_back(node, costate):
    return few_rows(costate, matrix_parts(node), NT) + node[2]


def kernel(
    seq_count,
    features_hbm,
    path_hbm,
    initial_hbm,
    cotan_hbm,
    in_weight_hbm,
    weight_hbm,
    bias_hbm,
    state_out,
    adjoint_out,
    features_ref,
    path_ref,
    initial_ref,
    cotan_ref,
    in_weight_ref,
    weight_ref,
    bias_ref,
    fetch_sems,
    previous_ref,
    keep_ref,
    term_ref,
    offset_ref,
    map_ref,
    acc_ref,
    pair_ref,
    row_ref,
    ahead_ref,
    behind_ref,
    out_ahead_ref,
    out_behind_ref,
    row_sems,
    pair_send,
    pair_recv,
    ahead_sems,
    behind_sems,
):
    rows, width = path_hbm.shape
    blocks = rows // BLOCK
    me = lax.axis_index("seq")
    groups = seq_count // GROUP
    group = me // GROUP

    def at(place):
        return {"seq": place}

    fetches = []
    for source, target in (
        (path_hbm, path_ref),
        (features_hbm, features_ref),
        (in_weight_hbm, in_weight_ref),
        (bias_hbm, bias_ref),
        (weight_hbm, weight_ref),
        (initial_hbm, initial_ref),
        (cotan_hbm, cotan_ref),
    ):
        fetch = pltpu.make_async_copy(source, target, fetch_sems.at[len(fetches)])
        fetch.start()
        fetches.append(fetch)

    barrier = pltpu.get_barrier_semaphore()
    greeted = jnp.int32(0)
    for distance in (1, GROUP):

        @pl.when(me >= distance)
        def _():
            pl.semaphore_signal(barrier, inc=1, device_id=at(me - distance))

        @pl.when(me < seq_count - distance)
        def _():
            pl.semaphore_signal(barrier, inc=1, device_id=at(me + distance))

        greeted = greeted + jnp.where(me >= distance, 1, 0)
        greeted = greeted + jnp.where(me < seq_count - distance, 1, 0)
    sides = [(me // bit) % 2 for bit in GROUP_LEVELS]
    partners = [me + bit - 2 * bit * side for bit, side in zip(GROUP_LEVELS, sides)]
    for partner in partners[1:]:
        pl.semaphore_signal(barrier, inc=1, device_id=at(partner))
        greeted = greeted + 1
    pl.semaphore_wait(barrier, greeted)

    row_copy = pltpu.make_async_remote_copy(
        src_ref=path_hbm.at[pl.ds(rows - 8, 8)],
        dst_ref=row_ref,
        send_sem=row_sems.at[0],
        recv_sem=row_sems.at[1],
        device_id=at(me + 1),
    )

    @pl.when(me < seq_count - 1)
    def _():
        row_copy.start()

    for fetch in fetches[:4]:
        fetch.wait()

    projected = (
        product(features_ref[...], in_weight_ref[...])
        + bias_ref[...][None, :]
    )
    previous_ref[pl.ds(1, rows - 1), :] = path_ref[pl.ds(0, rows - 1), :]

    for fetch in fetches[4:]:
        fetch.wait()

    @pl.when(me > 0)
    def _():
        row_copy.wait_recv()
        previous_ref[pl.ds(0, 1), :] = row_ref[pl.ds(7, 1), :]

    @pl.when(me == 0)
    def _():
        previous_ref[pl.ds(0, 1), :] = initial_ref[...]

    previous = previous_ref[...]
    weight_parts = split(weight_ref[...])
    recurrent = product_of_parts(split(previous), weight_parts)
    reset_gate = jax.nn.sigmoid(projected[:, :width] + recurrent[:, :width])
    write_gate = jax.nn.sigmoid(
        projected[:, width : 2 * width] + recurrent[:, width : 2 * width]
    )
    cand_recurrent = recurrent[:, 2 * width :]
    candidate = jnp.tanh(projected[:, 2 * width :] + reset_gate * cand_recurrent)
    updated = previous + write_gate * (candidate - previous)
    keep_rate = 1.0 - write_gate
    slopes = write_gate * (1.0 - candidate * candidate)
    reset_terms = slopes * cand_recurrent * reset_gate * (1.0 - reset_gate)
    write_terms = (candidate - previous) * write_gate * (1.0 - write_gate)
    cand_terms = slopes * reset_gate
    keep_ref[...] = keep_rate
    term_ref[0] = reset_terms
    term_ref[1] = write_terms
    term_ref[2] = cand_terms
    offset_ref[...] = (
        updated
        - keep_rate * previous
        - reset_terms * recurrent[:, :width]
        - write_terms * recurrent[:, width : 2 * width]
        - cand_terms * cand_recurrent
    )

    def coupling(row):
        total = weight_ref[:, pl.ds(0, width)] * term_ref[0, pl.ds(row, 1), :]
        for part in (1, 2):
            columns = pl.ds(part * width, width)
            total = total + weight_ref[:, columns] * term_ref[part, pl.ds(row, 1), :]
        return total

    diagonal = lax.broadcasted_iota(jnp.int32, (width, width), 0) == lax.broadcasted_iota(
        jnp.int32, (width, width), 1
    )
    for block in range(blocks):
        row = block * BLOCK
        first = coupling(row) + jnp.where(diagonal, keep_ref[pl.ds(row, 1), :], 0.0)
        map_ref[block, pl.ds(0, width), :] = first
        map_ref[block, pl.ds(width, PAD), :] = jnp.broadcast_to(
            offset_ref[pl.ds(row, 1), :], (PAD, width)
        )
        acc_ref[block] = first * cotan_ref[pl.ds(row, 1), :]

    def gather_step(step, carry):
        for block in range(blocks):
            row = block * BLOCK + step
            mapped = map_ref[block]
            moved = mapped * keep_ref[pl.ds(row, 1), :] + product(mapped, coupling(row))
            map_ref[block, pl.ds(0, width), :] = moved[:width]
            map_ref[block, pl.ds(width, PAD), :] = moved[width:] + offset_ref[pl.ds(row, 1), :]
            acc_ref[block] += moved[:width] * cotan_ref[pl.ds(row, 1), :]
        return carry

    lax.fori_loop(1, BLOCK, gather_step, 0)

    levels = [[node_of(map_ref[block], row_sums(acc_ref[block])) for block in range(blocks)]]
    while len(levels[-1]) > 1:
        nodes = levels[-1]
        levels.append([merge(nodes[i], nodes[i + 1]) for i in range(0, len(nodes), 2)])

    node = levels[-1][0]
    tall = width + 2 * SENT
    half = tall // 2

    def write_message(target, node):
        target[pl.ds(0, width + SENT), :] = node[0][: width + SENT]
        target[pl.ds(width + SENT, SENT), :] = node[2][:SENT]

    def read_message(source):
        offset = source[pl.ds(width, SENT), :]
        adjoint = source[pl.ds(width + SENT, SENT), :]
        return node_of(
            jnp.concatenate([source[pl.ds(0, width), :], offset, offset], axis=0),
            jnp.concatenate([adjoint, adjoint], axis=0),
        )

    def send(ref, index, partner):
        copy = pltpu.make_async_remote_copy(
            src_ref=ref,
            dst_ref=ref,
            send_sem=pair_send.at[index],
            recv_sem=pair_recv.at[index],
            device_id=at(partner),
        )
        copy.start()
        return copy

    pairs = []
    write_message(pair_ref.at[0, sides[0]], node)
    sibling_copy = send(pair_ref.at[0, sides[0]], 0, partners[0])
    sibling_copy.wait_recv()
    pairs.append([read_message(pair_ref.at[0, i]) for i in (0, 1)])
    node = merge(*pairs[0])

    write_message(pair_ref.at[1, sides[1]], node)
    my_half = pl.ds(pl.multiple_of(half * sides[0], SENT), half)
    half_copy = send(pair_ref.at[1, sides[1], my_half], 1, partners[1])
    half_copy.wait_recv()
    shared_copy = send(pair_ref.at[1, 1 - sides[1], my_half], 2, partners[0])
    shared_copy.wait_recv()
    pairs.append([read_message(pair_ref.at[1, i]) for i in (0, 1)])
    node = merge(*pairs[1])
    copies = [sibling_copy, half_copy, shared_copy]

    ahead_copy = pltpu.make_async_remote_copy(
        src_ref=out_ahead_ref,
        dst_ref=ahead_ref,
        send_sem=ahead_sems.at[0],
        recv_sem=ahead_sems.at[1],
        device_id=at(me + GROUP),
    )
    behind_copy = pltpu.make_async_remote_copy(
        src_ref=out_behind_ref,
        dst_ref=behind_ref,
        send_sem=behind_sems.at[0],
        recv_sem=behind_sems.at[1],
        device_id=at(me - GROUP),
    )

    def doubled(ref):
        return jnp.concatenate([ref[...], ref[...]], axis=0)

    def pass_forward():
        @pl.when(group == 0)
        def _():
            ahead_ref[...] = jnp.broadcast_to(initial_ref[...], ahead_ref.shape)

        @pl.when(group > 0)
        def _():
            ahead_copy.wait_recv()

        @pl.when(group < groups - 1)
        def _():
            out_ahead_ref[...] = go_forward(node, doubled(ahead_ref))[:SENT]
            ahead_copy.start()

    def pass_back():
        @pl.when(group == groups - 1)
        def _():
            behind_ref[...] = jnp.zeros_like(behind_ref)
            out_behind_ref[...] = node[2][:SENT]

        @pl.when(group < groups - 1)
        def _():
            behind_copy.wait_recv()

            out_behind_ref[...] = go_back(node, doubled(behind_ref))[:SENT]

        @pl.when(group > 0)
        def _():
            behind_copy.start()

    @pl.when(group < groups // 2)
    def _():
        pass_forward()
        pass_back()

    @pl.when(group >= groups // 2)
    def _():
        pass_back()
        pass_forward()

    state = doubled(ahead_ref)
    costate = doubled(behind_ref)
    for level in reversed(range(len(GROUP_LEVELS))):
        early, late = pairs[level]
        is_late = sides[level] == 1
        state, costate = (
            jnp.where(is_late, go_forward(early, state), state),
            jnp.where(is_late, costate, go_back(late, costate)),
        )

    entries = [(state, costate)]
    for nodes in reversed(levels[:-1]):
        finer = []
        for i, (state, costate) in enumerate(entries):
            early, late = nodes[2 * i], nodes[2 * i + 1]
            finer.append((state, go_back(late, costate)))
            finer.append((go_forward(early, state), costate))
        entries = finer

    states = jnp.concatenate([entry[0][:1] for entry in entries], axis=0)
    costates = jnp.concatenate([entry[1][:1] for entry in entries], axis=0)

    def apply_step(step, carry):
        states, costates = carry
        now = pl.ds(step, blocks, stride=BLOCK)
        mapped = few_rows(states, weight_parts, NN)
        states = keep_ref[now, :] * states + offset_ref[now, :]
        for part in range(3):
            columns = slice(part * width, (part + 1) * width)
            states = states + term_ref[part, now, :] * mapped[:, columns]
        state_out[now, :] = states

        back = pl.ds(BLOCK - 1 - step, blocks, stride=BLOCK)
        costates = cotan_ref[back, :] + costates
        adjoint_out[back, :] = costates
        spread = jnp.concatenate(
            [term_ref[part, back, :] * costates for part in range(3)], axis=1
        )
        costates = keep_ref[back, :] * costates + few_rows(spread, weight_parts, NT)
        return states, costates

    lax.fori_loop(0, BLOCK, apply_step, (states, costates))

    @pl.when(me < seq_count - 1)
    def _():
        row_copy.wait_send()

    for copy in copies:
        copy.wait_send()

    @pl.when(group < groups - 1)
    def _():
        ahead_copy.wait_send()

    @pl.when(group > 0)
    def _():
        behind_copy.wait_send()


def per_device(
    seq_count, inputs, trajectory, initial_state, cotangent, in_weight, recurrent_weight, gate_bias
):
    rows, width = trajectory.shape[1:]
    blocks = rows // BLOCK
    out = jax.ShapeDtypeStruct((rows, width), jnp.float32)
    tall = width + PAD
    vmem = functools.partial(pltpu.VMEM, dtype=jnp.float32)
    pair_sems = pltpu.SemaphoreType.DMA((2,))
    new_state, adjoint = pl.pallas_call(
        functools.partial(kernel, seq_count),
        out_shape=(out, out),
        in_specs=[pl.BlockSpec(memory_space=pltpu.HBM)] * 7,
        out_specs=(pl.BlockSpec(memory_space=pltpu.VMEM),) * 2,
        scratch_shapes=[
            vmem(inputs.shape[1:]),
            vmem((rows, width)),
            vmem((1, width)),
            vmem((rows, width)),
            vmem(in_weight.shape),
            vmem(recurrent_weight.shape),
            vmem((3 * width,)),
            pltpu.SemaphoreType.DMA((7,)),
            vmem((rows, width)),
            vmem((rows, width)),
            vmem((3, rows, width)),
            vmem((rows, width)),
            vmem((blocks, tall, width)),
            vmem((blocks, width, width)),
            vmem((len(GROUP_LEVELS), 2, width + 2 * SENT, width)),
            vmem((8, width)),
            vmem((SENT, width)),
            vmem((SENT, width)),
            vmem((SENT, width)),
            vmem((SENT, width)),
            pair_sems,
            pltpu.SemaphoreType.DMA((3,)),
            pltpu.SemaphoreType.DMA((3,)),
            pair_sems,
            pair_sems,
        ],
        compiler_params=pltpu.CompilerParams(
            collective_id=0, has_side_effects=True, vmem_limit_bytes=64 * 1024 * 1024
        ),
        name="newton_step",
    )(
        inputs[0],
        trajectory[0],
        initial_state,
        cotangent[0],
        in_weight,
        recurrent_weight,
        gate_bias,
    )
    return new_state[None], adjoint[None]


def solution(mesh):
    return jax.shard_map(
        functools.partial(per_device, mesh.shape["seq"]),
        mesh=mesh,
        in_specs=(
            P("dp", "seq", None),
            P("dp", "seq", None),
            P("dp", None),
            P("dp", "seq", None),
            P(),
            P(),
            P(),
        ),
        out_specs=(P("dp", "seq", None), P("dp", "seq", None)),
        check_vma=False,
    )
```

```python
import functools

import jax
import jax.numpy as jnp
from jax import lax
from jax.experimental import pallas as pl
from jax.experimental.pallas import tpu as pltpu
from jax.sharding import PartitionSpec as P

BLOCK = 8
GROUP_LEVELS = (1, 2)
GROUP = 4
PAD = 16
SENT = 8

NT = (((1,), (1,)), ((), ()))
NN = (((1,), (0,)), ((), ()))


def split(value):
    high = value.astype(jnp.bfloat16)
    low = (value - high.astype(jnp.float32)).astype(jnp.bfloat16)
    return high, low


def product_of_parts(rows, weights):
    (high, low), (w_high, w_low) = rows, weights
    width = w_high.shape[1]
    stacked = jnp.concatenate(
        [
            jnp.concatenate([w_high, w_low], axis=1),
            jnp.concatenate([w_high, jnp.zeros_like(w_low)], axis=1),
        ],
        axis=0,
    )
    out = jnp.dot(
        jnp.concatenate([high, low], axis=1), stacked, preferred_element_type=jnp.float32
    )
    return out[:, :width] + out[:, width:]


def product(rows, weights):
    return product_of_parts(split(rows), split(weights))


def few_rows(rows, parts, dims):
    count = rows.shape[0]
    side = 1 - dims[0][1][0]
    width = parts[0].shape[side]
    out = lax.dot_general(
        jnp.concatenate(split(rows), axis=0),
        jnp.concatenate(parts, axis=side),
        dims,
        preferred_element_type=jnp.float32,
    )
    return out[:count, :width] + out[count:, :width] + out[:count, width:]


def row_sums(matrix):
    ones = jnp.ones((PAD, 2 * matrix.shape[1]), jnp.bfloat16)
    return lax.dot_general(
        ones,
        jnp.concatenate(split(matrix), axis=1),
        NT,
        preferred_element_type=jnp.float32,
    )


def node_of(mapped, adjoint):
    return mapped, split(mapped), adjoint


def matrix_parts(node):
    width = node[0].shape[1]
    return tuple(part[:width] for part in node[1])


def merge(early, late):
    width = early[0].shape[1]
    merged = product_of_parts(early[1], matrix_parts(late))
    merged = jnp.concatenate([merged[:width], merged[width:] + late[0][width:]], axis=0)
    return node_of(merged, early[2] + few_rows(late[2], matrix_parts(early), NT))


def go_forward(node, state):
    return few_rows(state, matrix_parts(node), NN) + node[0][state.shape[1] :]


def go_back(node, costate):
    return few_rows(costate, matrix_parts(node), NT) + node[2]


def kernel(
    seq_count,
    features_hbm,
    path_hbm,
    initial_hbm,
    cotan_hbm,
    in_weight_hbm,
    weight_hbm,
    bias_hbm,
    state_out,
    adjoint_out,
    features_ref,
    path_ref,
    initial_ref,
    cotan_ref,
    in_weight_ref,
    weight_ref,
    bias_ref,
    fetch_sems,
    previous_ref,
    keep_ref,
    term_ref,
    offset_ref,
    map_ref,
    acc_ref,
    pair_ref,
    row_ref,
    ahead_ref,
    behind_ref,
    out_ahead_ref,
    out_behind_ref,
    entry_ref,
    row_sems,
    pair_send,
    pair_recv,
    ahead_sems,
    behind_sems,
):
    rows, width = path_hbm.shape
    blocks = rows // BLOCK
    me = lax.axis_index("seq")
    groups = seq_count // GROUP
    group = me // GROUP

    def at(place):
        return {"seq": place}

    fetches = []
    for source, target in (
        (path_hbm, path_ref),
        (features_hbm, features_ref),
        (in_weight_hbm, in_weight_ref),
        (bias_hbm, bias_ref),
        (weight_hbm, weight_ref),
        (initial_hbm, initial_ref),
        (cotan_hbm, cotan_ref),
    ):
        fetch = pltpu.make_async_copy(source, target, fetch_sems.at[len(fetches)])
        fetch.start()
        fetches.append(fetch)

    barrier = pltpu.get_barrier_semaphore()
    greeted = jnp.int32(0)
    for distance in (1, GROUP):

        @pl.when(me >= distance)
        def _():
            pl.semaphore_signal(barrier, inc=1, device_id=at(me - distance))

        @pl.when(me < seq_count - distance)
        def _():
            pl.semaphore_signal(barrier, inc=1, device_id=at(me + distance))

        greeted = greeted + jnp.where(me >= distance, 1, 0)
        greeted = greeted + jnp.where(me < seq_count - distance, 1, 0)
    sides = [(me // bit) % 2 for bit in GROUP_LEVELS]
    partners = [me + bit - 2 * bit * side for bit, side in zip(GROUP_LEVELS, sides)]
    for partner in partners[1:]:
        pl.semaphore_signal(barrier, inc=1, device_id=at(partner))
        greeted = greeted + 1
    pl.semaphore_wait(barrier, greeted)

    row_copy = pltpu.make_async_remote_copy(
        src_ref=path_hbm.at[pl.ds(rows - 8, 8)],
        dst_ref=row_ref,
        send_sem=row_sems.at[0],
        recv_sem=row_sems.at[1],
        device_id=at(me + 1),
    )

    @pl.when(me < seq_count - 1)
    def _():
        row_copy.start()

    for fetch in fetches[:4]:
        fetch.wait()

    projected = (
        product(features_ref[...], in_weight_ref[...])
        + bias_ref[...][None, :]
    )
    previous_ref[pl.ds(1, rows - 1), :] = path_ref[pl.ds(0, rows - 1), :]

    for fetch in fetches[4:]:
        fetch.wait()

    @pl.when(me > 0)
    def _():
        row_copy.wait_recv()
        previous_ref[pl.ds(0, 1), :] = row_ref[pl.ds(7, 1), :]

    @pl.when(me == 0)
    def _():
        previous_ref[pl.ds(0, 1), :] = initial_ref[...]

    previous = previous_ref[...]
    weight_parts = split(weight_ref[...])
    recurrent = product_of_parts(split(previous), weight_parts)
    reset_gate = jax.nn.sigmoid(projected[:, :width] + recurrent[:, :width])
    write_gate = jax.nn.sigmoid(
        projected[:, width : 2 * width] + recurrent[:, width : 2 * width]
    )
    cand_recurrent = recurrent[:, 2 * width :]
    candidate = jnp.tanh(projected[:, 2 * width :] + reset_gate * cand_recurrent)
    updated = previous + write_gate * (candidate - previous)
    keep_rate = 1.0 - write_gate
    slopes = write_gate * (1.0 - candidate * candidate)
    reset_terms = slopes * cand_recurrent * reset_gate * (1.0 - reset_gate)
    write_terms = (candidate - previous) * write_gate * (1.0 - write_gate)
    cand_terms = slopes * reset_gate
    keep_ref[...] = keep_rate
    term_ref[0] = reset_terms
    term_ref[1] = write_terms
    term_ref[2] = cand_terms
    offset_ref[...] = (
        updated
        - keep_rate * previous
        - reset_terms * recurrent[:, :width]
        - write_terms * recurrent[:, width : 2 * width]
        - cand_terms * cand_recurrent
    )

    def coupling(row):
        total = weight_ref[:, pl.ds(0, width)] * term_ref[0, pl.ds(row, 1), :]
        for part in (1, 2):
            columns = pl.ds(part * width, width)
            total = total + weight_ref[:, columns] * term_ref[part, pl.ds(row, 1), :]
        return total

    diagonal = lax.broadcasted_iota(jnp.int32, (width, width), 0) == lax.broadcasted_iota(
        jnp.int32, (width, width), 1
    )
    for block in range(blocks):
        row = block * BLOCK
        first = coupling(row) + jnp.where(diagonal, keep_ref[pl.ds(row, 1), :], 0.0)
        map_ref[block, pl.ds(0, width), :] = first
        map_ref[block, pl.ds(width, PAD), :] = jnp.broadcast_to(
            offset_ref[pl.ds(row, 1), :], (PAD, width)
        )
        acc_ref[block] = first * cotan_ref[pl.ds(row, 1), :]

    def gather_step(step, carry):
        for block in range(blocks):
            row = block * BLOCK + step
            mapped = map_ref[block]
            moved = mapped * keep_ref[pl.ds(row, 1), :] + product(mapped, coupling(row))
            map_ref[block, pl.ds(0, width), :] = moved[:width]
            map_ref[block, pl.ds(width, PAD), :] = moved[width:] + offset_ref[pl.ds(row, 1), :]
            acc_ref[block] += moved[:width] * cotan_ref[pl.ds(row, 1), :]
        return carry

    lax.fori_loop(1, BLOCK, gather_step, 0)

    levels = [[node_of(map_ref[block], row_sums(acc_ref[block])) for block in range(blocks)]]
    while len(levels[-1]) > 1:
        nodes = levels[-1]
        levels.append([merge(nodes[i], nodes[i + 1]) for i in range(0, len(nodes), 2)])

    node = levels[-1][0]
    tall = width + 2 * SENT

    def write_message(target, node):
        target[pl.ds(0, width + SENT), :] = node[0][: width + SENT]
        target[pl.ds(width + SENT, SENT), :] = node[2][:SENT]

    def read_message(source):
        offset = source[pl.ds(width, SENT), :]
        adjoint = source[pl.ds(width + SENT, SENT), :]
        return node_of(
            jnp.concatenate([source[pl.ds(0, width), :], offset, offset], axis=0),
            jnp.concatenate([adjoint, adjoint], axis=0),
        )

    def send(ref, index, partner):
        copy = pltpu.make_async_remote_copy(
            src_ref=ref,
            dst_ref=ref,
            send_sem=pair_send.at[index],
            recv_sem=pair_recv.at[index],
            device_id=at(partner),
        )
        copy.start()
        return copy

    pairs = []
    write_message(pair_ref.at[0, sides[0]], node)
    sibling_copy = send(pair_ref.at[0, sides[0]], 0, partners[0])
    sibling_copy.wait_recv()
    pairs.append([read_message(pair_ref.at[0, i]) for i in (0, 1)])

    ahead_copy = pltpu.make_async_remote_copy(
        src_ref=out_ahead_ref,
        dst_ref=ahead_ref,
        send_sem=ahead_sems.at[0],
        recv_sem=ahead_sems.at[1],
        device_id=at(me + GROUP),
    )
    behind_copy = pltpu.make_async_remote_copy(
        src_ref=out_behind_ref,
        dst_ref=behind_ref,
        send_sem=behind_sems.at[0],
        recv_sem=behind_sems.at[1],
        device_id=at(me - GROUP),
    )
    entry_copy = pltpu.make_async_remote_copy(
        src_ref=entry_ref,
        dst_ref=entry_ref,
        send_sem=pair_send.at[2],
        recv_sem=pair_recv.at[2],
        device_id=at(partners[0]),
    )

    def doubled(rows):
        return jnp.concatenate([rows, rows], axis=0)

    @pl.when(sides[0] == 1)
    def _():
        write_message(pair_ref.at[1, sides[1]], merge(*pairs[0]))
        plane_copy = send(pair_ref.at[1, sides[1]], 1, partners[1])
        plane_copy.wait_recv()
        early, late = [read_message(pair_ref.at[1, i]) for i in (0, 1)]
        node = merge(early, late)

        def pass_forward():
            @pl.when(group == 0)
            def _():
                ahead_ref[...] = jnp.broadcast_to(initial_ref[...], ahead_ref.shape)

            @pl.when(group > 0)
            def _():
                ahead_copy.wait_recv()

            @pl.when(group < groups - 1)
            def _():
                out_ahead_ref[...] = go_forward(node, doubled(ahead_ref[...]))[:SENT]
                ahead_copy.start()

        def pass_back():
            @pl.when(group == groups - 1)
            def _():
                behind_ref[...] = jnp.zeros_like(behind_ref)
                out_behind_ref[...] = node[2][:SENT]

            @pl.when(group < groups - 1)
            def _():
                behind_copy.wait_recv()
                out_behind_ref[...] = go_back(node, doubled(behind_ref[...]))[:SENT]

            @pl.when(group > 0)
            def _():
                behind_copy.start()

        @pl.when(group < groups // 2)
        def _():
            pass_forward()
            pass_back()

        @pl.when(group >= groups // 2)
        def _():
            pass_back()
            pass_forward()

        state, costate = doubled(ahead_ref[...]), doubled(behind_ref[...])
        is_late = sides[1] == 1
        entry_ref[pl.ds(0, SENT), :] = jnp.where(is_late, go_forward(early, state), state)[:SENT]
        entry_ref[pl.ds(SENT, SENT), :] = jnp.where(is_late, costate, go_back(late, costate))[
            :SENT
        ]
        entry_copy.start()
        plane_copy.wait_send()

        @pl.when(group < groups - 1)
        def _():
            ahead_copy.wait_send()

        @pl.when(group > 0)
        def _():
            behind_copy.wait_send()

    @pl.when(sides[0] == 0)
    def _():
        entry_copy.wait_recv()

    state = doubled(entry_ref[pl.ds(0, SENT), :])
    costate = doubled(entry_ref[pl.ds(SENT, SENT), :])
    early, late = pairs[0]
    is_late = sides[0] == 1
    state, costate = (
        jnp.where(is_late, go_forward(early, state), state),
        jnp.where(is_late, costate, go_back(late, costate)),
    )

    entries = [(state, costate)]
    for nodes in reversed(levels[:-1]):
        finer = []
        for i, (state, costate) in enumerate(entries):
            early, late = nodes[2 * i], nodes[2 * i + 1]
            finer.append((state, go_back(late, costate)))
            finer.append((go_forward(early, state), costate))
        entries = finer

    states = jnp.concatenate([entry[0][:1] for entry in entries], axis=0)
    costates = jnp.concatenate([entry[1][:1] for entry in entries], axis=0)

    def apply_step(step, carry):
        states, costates = carry
        now = pl.ds(step, blocks, stride=BLOCK)
        mapped = few_rows(states, weight_parts, NN)
        states = keep_ref[now, :] * states + offset_ref[now, :]
        for part in range(3):
            columns = slice(part * width, (part + 1) * width)
            states = states + term_ref[part, now, :] * mapped[:, columns]
        state_out[now, :] = states

        back = pl.ds(BLOCK - 1 - step, blocks, stride=BLOCK)
        costates = cotan_ref[back, :] + costates
        adjoint_out[back, :] = costates
        spread = jnp.concatenate(
            [term_ref[part, back, :] * costates for part in range(3)], axis=1
        )
        costates = keep_ref[back, :] * costates + few_rows(spread, weight_parts, NT)
        return states, costates

    lax.fori_loop(0, BLOCK, apply_step, (states, costates))

    @pl.when(me < seq_count - 1)
    def _():
        row_copy.wait_send()

    sibling_copy.wait_send()

    @pl.when(sides[0] == 1)
    def _():
        entry_copy.wait_send()


def per_device(
    seq_count, inputs, trajectory, initial_state, cotangent, in_weight, recurrent_weight, gate_bias
):
    rows, width = trajectory.shape[1:]
    blocks = rows // BLOCK
    out = jax.ShapeDtypeStruct((rows, width), jnp.float32)
    tall = width + PAD
    vmem = functools.partial(pltpu.VMEM, dtype=jnp.float32)
    pair_sems = pltpu.SemaphoreType.DMA((2,))
    new_state, adjoint = pl.pallas_call(
        functools.partial(kernel, seq_count),
        out_shape=(out, out),
        in_specs=[pl.BlockSpec(memory_space=pltpu.HBM)] * 7,
        out_specs=(pl.BlockSpec(memory_space=pltpu.VMEM),) * 2,
        scratch_shapes=[
            vmem(inputs.shape[1:]),
            vmem((rows, width)),
            vmem((1, width)),
            vmem((rows, width)),
            vmem(in_weight.shape),
            vmem(recurrent_weight.shape),
            vmem((3 * width,)),
            pltpu.SemaphoreType.DMA((7,)),
            vmem((rows, width)),
            vmem((rows, width)),
            vmem((3, rows, width)),
            vmem((rows, width)),
            vmem((blocks, tall, width)),
            vmem((blocks, width, width)),
            vmem((len(GROUP_LEVELS), 2, width + 2 * SENT, width)),
            vmem((8, width)),
            vmem((SENT, width)),
            vmem((SENT, width)),
            vmem((SENT, width)),
            vmem((SENT, width)),
            vmem((2 * SENT, width)),
            pair_sems,
            pltpu.SemaphoreType.DMA((3,)),
            pltpu.SemaphoreType.DMA((3,)),
            pair_sems,
            pair_sems,
        ],
        compiler_params=pltpu.CompilerParams(
            collective_id=0, has_side_effects=True, vmem_limit_bytes=64 * 1024 * 1024
        ),
        name="newton_step",
    )(
        inputs[0],
        trajectory[0],
        initial_state,
        cotangent[0],
        in_weight,
        recurrent_weight,
        gate_bias,
    )
    return new_state[None], adjoint[None]


def solution(mesh):
    return jax.shard_map(
        functools.partial(per_device, mesh.shape["seq"]),
        mesh=mesh,
        in_specs=(
            P("dp", "seq", None),
            P("dp", "seq", None),
            P("dp", None),
            P("dp", "seq", None),
            P(),
            P(),
            P(),
        ),
        out_specs=(P("dp", "seq", None), P("dp", "seq", None)),
        check_vma=False,
    )
```

```python
import functools

import jax
import jax.numpy as jnp
from jax import lax
from jax.experimental import pallas as pl
from jax.experimental.pallas import tpu as pltpu
from jax.sharding import PartitionSpec as P

BLOCK = 8
GROUP_LEVELS = (1, 2)
GROUP = 4
PAD = 16
SENT = 8

NT = (((1,), (1,)), ((), ()))
NN = (((1,), (0,)), ((), ()))


def split(value):
    high = value.astype(jnp.bfloat16)
    low = (value - high.astype(jnp.float32)).astype(jnp.bfloat16)
    return high, low


def product_of_parts(rows, weights):
    (high, low), (w_high, w_low) = rows, weights
    width = w_high.shape[1]
    stacked = jnp.concatenate(
        [
            jnp.concatenate([w_high, w_low], axis=1),
            jnp.concatenate([w_high, jnp.zeros_like(w_low)], axis=1),
        ],
        axis=0,
    )
    out = jnp.dot(
        jnp.concatenate([high, low], axis=1), stacked, preferred_element_type=jnp.float32
    )
    return out[:, :width] + out[:, width:]


def product(rows, weights):
    return product_of_parts(split(rows), split(weights))


def few_rows(rows, parts, dims):
    count = rows.shape[0]
    side = 1 - dims[0][1][0]
    width = parts[0].shape[side]
    out = lax.dot_general(
        jnp.concatenate(split(rows), axis=0),
        jnp.concatenate(parts, axis=side),
        dims,
        preferred_element_type=jnp.float32,
    )
    return out[:count, :width] + out[count:, :width] + out[:count, width:]


def row_sums(matrix):
    ones = jnp.ones((PAD, 2 * matrix.shape[1]), jnp.bfloat16)
    return lax.dot_general(
        ones,
        jnp.concatenate(split(matrix), axis=1),
        NT,
        preferred_element_type=jnp.float32,
    )


def node_of(mapped, adjoint):
    return mapped, split(mapped), adjoint


def matrix_parts(node):
    width = node[0].shape[1]
    return tuple(part[:width] for part in node[1])


def merge(early, late):
    width = early[0].shape[1]
    merged = product_of_parts(early[1], matrix_parts(late))
    merged = jnp.concatenate([merged[:width], merged[width:] + late[0][width:]], axis=0)
    return node_of(merged, early[2] + few_rows(late[2], matrix_parts(early), NT))


def go_forward(node, state):
    return few_rows(state, matrix_parts(node), NN) + node[0][state.shape[1] :]


def go_back(node, costate):
    return few_rows(costate, matrix_parts(node), NT) + node[2]


def kernel(
    seq_count,
    features_hbm,
    path_hbm,
    initial_hbm,
    cotan_hbm,
    in_weight_hbm,
    weight_hbm,
    bias_hbm,
    state_out,
    adjoint_out,
    features_ref,
    path_ref,
    initial_ref,
    cotan_ref,
    in_weight_ref,
    weight_ref,
    bias_ref,
    fetch_sems,
    previous_ref,
    keep_ref,
    term_ref,
    offset_ref,
    map_ref,
    acc_ref,
    pair_ref,
    row_ref,
    ahead_ref,
    behind_ref,
    out_ahead_ref,
    out_behind_ref,
    entry_ref,
    row_sems,
    pair_send,
    pair_recv,
    ahead_sems,
    behind_sems,
):
    rows, width = path_hbm.shape
    blocks = rows // BLOCK
    me = lax.axis_index("seq")
    groups = seq_count // GROUP
    group = me // GROUP
    odd, couple = group % 2, group // 2
    after = groups // 2 - 1 - couple
    neighbour = me + GROUP - 2 * GROUP * odd

    def at(place):
        return {"seq": place}

    fetches = []
    for source, target in (
        (path_hbm, path_ref),
        (features_hbm, features_ref),
        (in_weight_hbm, in_weight_ref),
        (bias_hbm, bias_ref),
        (weight_hbm, weight_ref),
        (initial_hbm, initial_ref),
        (cotan_hbm, cotan_ref),
    ):
        fetch = pltpu.make_async_copy(source, target, fetch_sems.at[len(fetches)])
        fetch.start()
        fetches.append(fetch)

    barrier = pltpu.get_barrier_semaphore()
    greeted = jnp.int32(0)
    for distance in (1, GROUP, 2 * GROUP):

        @pl.when(me >= distance)
        def _():
            pl.semaphore_signal(barrier, inc=1, device_id=at(me - distance))

        @pl.when(me < seq_count - distance)
        def _():
            pl.semaphore_signal(barrier, inc=1, device_id=at(me + distance))

        greeted = greeted + jnp.where(me >= distance, 1, 0)
        greeted = greeted + jnp.where(me < seq_count - distance, 1, 0)
    sides = [(me // bit) % 2 for bit in GROUP_LEVELS]
    partners = [me + bit - 2 * bit * side for bit, side in zip(GROUP_LEVELS, sides)]
    for partner in partners[1:]:
        pl.semaphore_signal(barrier, inc=1, device_id=at(partner))
        greeted = greeted + 1
    pl.semaphore_wait(barrier, greeted)

    row_copy = pltpu.make_async_remote_copy(
        src_ref=path_hbm.at[pl.ds(rows - 8, 8)],
        dst_ref=row_ref,
        send_sem=row_sems.at[0],
        recv_sem=row_sems.at[1],
        device_id=at(me + 1),
    )

    @pl.when(me < seq_count - 1)
    def _():
        row_copy.start()

    for fetch in fetches[:4]:
        fetch.wait()

    projected = (
        product(features_ref[...], in_weight_ref[...])
        + bias_ref[...][None, :]
    )
    previous_ref[pl.ds(1, rows - 1), :] = path_ref[pl.ds(0, rows - 1), :]

    for fetch in fetches[4:]:
        fetch.wait()

    @pl.when(me > 0)
    def _():
        row_copy.wait_recv()
        previous_ref[pl.ds(0, 1), :] = row_ref[pl.ds(7, 1), :]

    @pl.when(me == 0)
    def _():
        previous_ref[pl.ds(0, 1), :] = initial_ref[...]

    previous = previous_ref[...]
    weight_parts = split(weight_ref[...])
    recurrent = product_of_parts(split(previous), weight_parts)
    reset_gate = jax.nn.sigmoid(projected[:, :width] + recurrent[:, :width])
    write_gate = jax.nn.sigmoid(
        projected[:, width : 2 * width] + recurrent[:, width : 2 * width]
    )
    cand_recurrent = recurrent[:, 2 * width :]
    candidate = jnp.tanh(projected[:, 2 * width :] + reset_gate * cand_recurrent)
    updated = previous + write_gate * (candidate - previous)
    keep_rate = 1.0 - write_gate
    slopes = write_gate * (1.0 - candidate * candidate)
    reset_terms = slopes * cand_recurrent * reset_gate * (1.0 - reset_gate)
    write_terms = (candidate - previous) * write_gate * (1.0 - write_gate)
    cand_terms = slopes * reset_gate
    keep_ref[...] = keep_rate
    term_ref[0] = reset_terms
    term_ref[1] = write_terms
    term_ref[2] = cand_terms
    offset_ref[...] = (
        updated
        - keep_rate * previous
        - reset_terms * recurrent[:, :width]
        - write_terms * recurrent[:, width : 2 * width]
        - cand_terms * cand_recurrent
    )

    def coupling(row):
        total = weight_ref[:, pl.ds(0, width)] * term_ref[0, pl.ds(row, 1), :]
        for part in (1, 2):
            columns = pl.ds(part * width, width)
            total = total + weight_ref[:, columns] * term_ref[part, pl.ds(row, 1), :]
        return total

    diagonal = lax.broadcasted_iota(jnp.int32, (width, width), 0) == lax.broadcasted_iota(
        jnp.int32, (width, width), 1
    )
    for block in range(blocks):
        row = block * BLOCK
        first = coupling(row) + jnp.where(diagonal, keep_ref[pl.ds(row, 1), :], 0.0)
        map_ref[block, pl.ds(0, width), :] = first
        map_ref[block, pl.ds(width, PAD), :] = jnp.broadcast_to(
            offset_ref[pl.ds(row, 1), :], (PAD, width)
        )
        acc_ref[block] = first * cotan_ref[pl.ds(row, 1), :]

    def gather_step(step, carry):
        for block in range(blocks):
            row = block * BLOCK + step
            mapped = map_ref[block]
            moved = mapped * keep_ref[pl.ds(row, 1), :] + product(mapped, coupling(row))
            map_ref[block, pl.ds(0, width), :] = moved[:width]
            map_ref[block, pl.ds(width, PAD), :] = moved[width:] + offset_ref[pl.ds(row, 1), :]
            acc_ref[block] += moved[:width] * cotan_ref[pl.ds(row, 1), :]
        return carry

    lax.fori_loop(1, BLOCK, gather_step, 0)

    levels = [[node_of(map_ref[block], row_sums(acc_ref[block])) for block in range(blocks)]]
    while len(levels[-1]) > 1:
        nodes = levels[-1]
        levels.append([merge(nodes[i], nodes[i + 1]) for i in range(0, len(nodes), 2)])

    node = levels[-1][0]
    tall = width + 2 * SENT

    def write_message(target, node):
        target[pl.ds(0, width + SENT), :] = node[0][: width + SENT]
        target[pl.ds(width + SENT, SENT), :] = node[2][:SENT]

    def read_message(source):
        offset = source[pl.ds(width, SENT), :]
        adjoint = source[pl.ds(width + SENT, SENT), :]
        return node_of(
            jnp.concatenate([source[pl.ds(0, width), :], offset, offset], axis=0),
            jnp.concatenate([adjoint, adjoint], axis=0),
        )

    def copy_to(ref, index, partner):
        return pltpu.make_async_remote_copy(
            src_ref=ref,
            dst_ref=ref,
            send_sem=pair_send.at[index],
            recv_sem=pair_recv.at[index],
            device_id=at(partner),
        )

    def send(ref, index, partner):
        copy = copy_to(ref, index, partner)
        copy.start()
        return copy

    pairs = []
    write_message(pair_ref.at[0, sides[0]], node)
    sibling_copy = send(pair_ref.at[0, sides[0]], 0, partners[0])
    sibling_copy.wait_recv()
    pairs.append([read_message(pair_ref.at[0, i]) for i in (0, 1)])

    def pass_to(source, target, sems, distance):
        return [
            pltpu.make_async_remote_copy(
                src_ref=source,
                dst_ref=target,
                send_sem=sems.at[turn - 1],
                recv_sem=sems.at[2],
                device_id=at(me + distance * turn),
            )
            for turn in (1, 2)
        ]

    ahead_copies = pass_to(out_ahead_ref, ahead_ref, ahead_sems, GROUP)
    behind_copies = pass_to(out_behind_ref, behind_ref, behind_sems, -GROUP)
    entry_copy = pltpu.make_async_remote_copy(
        src_ref=entry_ref,
        dst_ref=entry_ref,
        send_sem=pair_send.at[2],
        recv_sem=pair_recv.at[2],
        device_id=at(partners[0]),
    )

    def doubled(rows):
        return jnp.concatenate([rows, rows], axis=0)

    @pl.when(sides[0] == 1)
    def _():
        write_message(pair_ref.at[1, sides[1]], merge(*pairs[0]))
        plane_copy = send(pair_ref.at[1, sides[1]], 1, partners[1])
        plane_copy.wait_recv()
        early, late = [read_message(pair_ref.at[1, i]) for i in (0, 1)]
        node = merge(early, late)

        write_message(pair_ref.at[2, odd], node)
        offsets_copy = copy_to(pair_ref.at[2, odd, pl.ds(width, 2 * SENT)], 3, neighbour)
        matrix_copy = copy_to(pair_ref.at[2, odd, pl.ds(0, width)], 4, neighbour)
        offsets_copy.start()

        @pl.when(1 - odd + after > 0)
        def _():
            matrix_copy.start()

        def pass_forward():
            @pl.when(couple == 0)
            def _():
                ahead_ref[...] = jnp.broadcast_to(initial_ref[...], ahead_ref.shape)

            @pl.when(couple > 0)
            def _():
                ahead_copies[0].wait_recv()

            @pl.when(odd == 1)
            def _():
                offsets_copy.wait_recv()
                matrix_copy.wait_recv()
                state = go_forward(read_message(pair_ref.at[2, 0]), doubled(ahead_ref[...]))
                ahead_ref[...] = state[:SENT]

                @pl.when(after > 0)
                def _():
                    out_ahead_ref[...] = go_forward(node, state)[:SENT]
                    for copy in ahead_copies:
                        copy.start()

        def pass_back():
            @pl.when(after > 0)
            def _():
                behind_copies[0].wait_recv()

            @pl.when(after == 0)
            def _():
                behind_ref[...] = jnp.zeros_like(behind_ref)

            @pl.when(odd == 0)
            def _():
                offsets_copy.wait_recv()

                @pl.when(after > 0)
                def _():
                    matrix_copy.wait_recv()
                    behind_ref[...] = go_back(
                        read_message(pair_ref.at[2, 1]), doubled(behind_ref[...])
                    )[:SENT]

                @pl.when(after == 0)
                def _():
                    behind_ref[...] = pair_ref[2, 1, pl.ds(width + SENT, SENT), :]

                @pl.when(couple > 0)
                def _():
                    out_behind_ref[...] = go_back(node, doubled(behind_ref[...]))[:SENT]
                    for copy in behind_copies:
                        copy.start()

        @pl.when(group < groups // 2)
        def _():
            pass_forward()
            pass_back()

        @pl.when(group >= groups // 2)
        def _():
            pass_back()
            pass_forward()

        state, costate = doubled(ahead_ref[...]), doubled(behind_ref[...])
        is_late = sides[1] == 1
        entry_ref[pl.ds(0, SENT), :] = jnp.where(is_late, go_forward(early, state), state)[:SENT]
        entry_ref[pl.ds(SENT, SENT), :] = jnp.where(is_late, costate, go_back(late, costate))[
            :SENT
        ]
        entry_copy.start()
        plane_copy.wait_send()
        offsets_copy.wait_send()

        @pl.when(1 - odd + after > 0)
        def _():
            matrix_copy.wait_send()

        @pl.when(odd * after > 0)
        def _():
            for copy in ahead_copies:
                copy.wait_send()

        @pl.when((1 - odd) * couple > 0)
        def _():
            for copy in behind_copies:
                copy.wait_send()

    @pl.when(sides[0] == 0)
    def _():
        entry_copy.wait_recv()

    state = doubled(entry_ref[pl.ds(0, SENT), :])
    costate = doubled(entry_ref[pl.ds(SENT, SENT), :])
    early, late = pairs[0]
    is_late = sides[0] == 1
    state, costate = (
        jnp.where(is_late, go_forward(early, state), state),
        jnp.where(is_late, costate, go_back(late, costate)),
    )

    entries = [(state, costate)]
    for nodes in reversed(levels[:-1]):
        finer = []
        for i, (state, costate) in enumerate(entries):
            early, late = nodes[2 * i], nodes[2 * i + 1]
            finer.append((state, go_back(late, costate)))
            finer.append((go_forward(early, state), costate))
        entries = finer

    states = jnp.concatenate([entry[0][:1] for entry in entries], axis=0)
    costates = jnp.concatenate([entry[1][:1] for entry in entries], axis=0)

    def apply_step(step, carry):
        states, costates = carry
        now = pl.ds(step, blocks, stride=BLOCK)
        mapped = few_rows(states, weight_parts, NN)
        states = keep_ref[now, :] * states + offset_ref[now, :]
        for part in range(3):
            columns = slice(part * width, (part + 1) * width)
            states = states + term_ref[part, now, :] * mapped[:, columns]
        state_out[now, :] = states

        back = pl.ds(BLOCK - 1 - step, blocks, stride=BLOCK)
        costates = cotan_ref[back, :] + costates
        adjoint_out[back, :] = costates
        spread = jnp.concatenate(
            [term_ref[part, back, :] * costates for part in range(3)], axis=1
        )
        costates = keep_ref[back, :] * costates + few_rows(spread, weight_parts, NT)
        return states, costates

    lax.fori_loop(0, BLOCK, apply_step, (states, costates))

    @pl.when(me < seq_count - 1)
    def _():
        row_copy.wait_send()

    sibling_copy.wait_send()

    @pl.when(sides[0] == 1)
    def _():
        entry_copy.wait_send()


def per_device(
    seq_count, inputs, trajectory, initial_state, cotangent, in_weight, recurrent_weight, gate_bias
):
    rows, width = trajectory.shape[1:]
    blocks = rows // BLOCK
    out = jax.ShapeDtypeStruct((rows, width), jnp.float32)
    tall = width + PAD
    vmem = functools.partial(pltpu.VMEM, dtype=jnp.float32)
    pair_sems = pltpu.SemaphoreType.DMA((2,))
    new_state, adjoint = pl.pallas_call(
        functools.partial(kernel, seq_count),
        out_shape=(out, out),
        in_specs=[pl.BlockSpec(memory_space=pltpu.HBM)] * 7,
        out_specs=(pl.BlockSpec(memory_space=pltpu.VMEM),) * 2,
        scratch_shapes=[
            vmem(inputs.shape[1:]),
            vmem((rows, width)),
            vmem((1, width)),
            vmem((rows, width)),
            vmem(in_weight.shape),
            vmem(recurrent_weight.shape),
            vmem((3 * width,)),
            pltpu.SemaphoreType.DMA((7,)),
            vmem((rows, width)),
            vmem((rows, width)),
            vmem((3, rows, width)),
            vmem((rows, width)),
            vmem((blocks, tall, width)),
            vmem((blocks, width, width)),
            vmem((len(GROUP_LEVELS) + 1, 2, width + 2 * SENT, width)),
            vmem((8, width)),
            vmem((SENT, width)),
            vmem((SENT, width)),
            vmem((SENT, width)),
            vmem((SENT, width)),
            vmem((2 * SENT, width)),
            pair_sems,
            pltpu.SemaphoreType.DMA((5,)),
            pltpu.SemaphoreType.DMA((5,)),
            pltpu.SemaphoreType.DMA((3,)),
            pltpu.SemaphoreType.DMA((3,)),
        ],
        compiler_params=pltpu.CompilerParams(
            collective_id=0, has_side_effects=True, vmem_limit_bytes=64 * 1024 * 1024
        ),
        name="newton_step",
    )(
        inputs[0],
        trajectory[0],
        initial_state,
        cotangent[0],
        in_weight,
        recurrent_weight,
        gate_bias,
    )
    return new_state[None], adjoint[None]


def solution(mesh):
    return jax.shard_map(
        functools.partial(per_device, mesh.shape["seq"]),
        mesh=mesh,
        in_specs=(
            P("dp", "seq", None),
            P("dp", "seq", None),
            P("dp", None),
            P("dp", "seq", None),
            P(),
            P(),
            P(),
        ),
        out_specs=(P("dp", "seq", None), P("dp", "seq", None)),
        check_vma=False,
    )
```

```python
import functools

import jax
import jax.numpy as jnp
from jax import lax
from jax.experimental import pallas as pl
from jax.experimental.pallas import tpu as pltpu
from jax.sharding import PartitionSpec as P

BLOCK = 8
GROUP_LEVELS = (1, 2)
GROUP = 4
PAD = 16
SENT = 8

NT = (((1,), (1,)), ((), ()))
NN = (((1,), (0,)), ((), ()))


def split(value):
    high = value.astype(jnp.bfloat16)
    low = (value - high.astype(jnp.float32)).astype(jnp.bfloat16)
    return high, low


def product_of_parts(rows, weights):
    (high, low), (w_high, w_low) = rows, weights
    width = w_high.shape[1]
    stacked = jnp.concatenate(
        [
            jnp.concatenate([w_high, w_low], axis=1),
            jnp.concatenate([w_high, jnp.zeros_like(w_low)], axis=1),
        ],
        axis=0,
    )
    out = jnp.dot(
        jnp.concatenate([high, low], axis=1), stacked, preferred_element_type=jnp.float32
    )
    return out[:, :width] + out[:, width:]


def product(rows, weights):
    return product_of_parts(split(rows), split(weights))


def few_rows(rows, parts, dims):
    count = rows.shape[0]
    side = 1 - dims[0][1][0]
    width = parts[0].shape[side]
    out = lax.dot_general(
        jnp.concatenate(split(rows), axis=0),
        jnp.concatenate(parts, axis=side),
        dims,
        preferred_element_type=jnp.float32,
    )
    return out[:count, :width] + out[count:, :width] + out[:count, width:]


def node_of(mapped, adjoint):
    return mapped, split(mapped), adjoint


def matrix_parts(node):
    width = node[0].shape[1]
    return tuple(part[:width] for part in node[1])


def merge(early, late):
    width = early[0].shape[1]
    merged = product_of_parts(early[1], matrix_parts(late))
    merged = jnp.concatenate([merged[:width], merged[width:] + late[0][width:]], axis=0)
    return node_of(merged, early[2] + few_rows(late[2], matrix_parts(early), NT))


def go_forward(node, state):
    return few_rows(state, matrix_parts(node), NN) + node[0][state.shape[1] :]


def go_back(node, costate):
    return few_rows(costate, matrix_parts(node), NT) + node[2]


def kernel(
    seq_count,
    features_hbm,
    path_hbm,
    initial_hbm,
    cotan_hbm,
    in_weight_hbm,
    weight_hbm,
    bias_hbm,
    state_out,
    adjoint_out,
    features_ref,
    path_ref,
    initial_ref,
    cotan_ref,
    in_weight_ref,
    weight_ref,
    bias_ref,
    fetch_sems,
    previous_ref,
    keep_ref,
    term_ref,
    offset_ref,
    map_ref,
    pair_ref,
    row_ref,
    ahead_ref,
    behind_ref,
    out_ahead_ref,
    out_behind_ref,
    entry_ref,
    row_sems,
    pair_send,
    pair_recv,
    ahead_sems,
    behind_sems,
):
    rows, width = path_hbm.shape
    blocks = rows // BLOCK
    me = lax.axis_index("seq")
    groups = seq_count // GROUP
    group = me // GROUP
    odd, couple = group % 2, group // 2
    after = groups // 2 - 1 - couple
    neighbour = me + GROUP - 2 * GROUP * odd

    def at(place):
        return {"seq": place}

    fetches = []
    for source, target in (
        (path_hbm, path_ref),
        (features_hbm, features_ref),
        (in_weight_hbm, in_weight_ref),
        (bias_hbm, bias_ref),
        (weight_hbm, weight_ref),
        (initial_hbm, initial_ref),
        (cotan_hbm, cotan_ref),
    ):
        fetch = pltpu.make_async_copy(source, target, fetch_sems.at[len(fetches)])
        fetch.start()
        fetches.append(fetch)

    barrier = pltpu.get_barrier_semaphore()
    greeted = jnp.int32(0)
    for distance in (1, GROUP, 2 * GROUP):

        @pl.when(me >= distance)
        def _():
            pl.semaphore_signal(barrier, inc=1, device_id=at(me - distance))

        @pl.when(me < seq_count - distance)
        def _():
            pl.semaphore_signal(barrier, inc=1, device_id=at(me + distance))

        greeted = greeted + jnp.where(me >= distance, 1, 0)
        greeted = greeted + jnp.where(me < seq_count - distance, 1, 0)
    sides = [(me // bit) % 2 for bit in GROUP_LEVELS]
    partners = [me + bit - 2 * bit * side for bit, side in zip(GROUP_LEVELS, sides)]
    for partner in partners[1:]:
        pl.semaphore_signal(barrier, inc=1, device_id=at(partner))
        greeted = greeted + 1
    pl.semaphore_wait(barrier, greeted)

    row_copy = pltpu.make_async_remote_copy(
        src_ref=path_hbm.at[pl.ds(rows - 8, 8)],
        dst_ref=row_ref,
        send_sem=row_sems.at[0],
        recv_sem=row_sems.at[1],
        device_id=at(me + 1),
    )

    @pl.when(me < seq_count - 1)
    def _():
        row_copy.start()

    for fetch in fetches[:4]:
        fetch.wait()

    projected = (
        product(features_ref[...], in_weight_ref[...])
        + bias_ref[...][None, :]
    )
    previous_ref[pl.ds(1, rows - 1), :] = path_ref[pl.ds(0, rows - 1), :]

    for fetch in fetches[4:]:
        fetch.wait()

    @pl.when(me > 0)
    def _():
        row_copy.wait_recv()
        previous_ref[pl.ds(0, 1), :] = row_ref[pl.ds(7, 1), :]

    @pl.when(me == 0)
    def _():
        previous_ref[pl.ds(0, 1), :] = initial_ref[...]

    previous = previous_ref[...]
    weight_parts = split(weight_ref[...])
    recurrent = product_of_parts(split(previous), weight_parts)
    reset_gate = jax.nn.sigmoid(projected[:, :width] + recurrent[:, :width])
    write_gate = jax.nn.sigmoid(
        projected[:, width : 2 * width] + recurrent[:, width : 2 * width]
    )
    cand_recurrent = recurrent[:, 2 * width :]
    candidate = jnp.tanh(projected[:, 2 * width :] + reset_gate * cand_recurrent)
    updated = previous + write_gate * (candidate - previous)
    keep_rate = 1.0 - write_gate
    slopes = write_gate * (1.0 - candidate * candidate)
    reset_terms = slopes * cand_recurrent * reset_gate * (1.0 - reset_gate)
    write_terms = (candidate - previous) * write_gate * (1.0 - write_gate)
    cand_terms = slopes * reset_gate
    keep_ref[...] = keep_rate
    term_ref[0] = reset_terms
    term_ref[1] = write_terms
    term_ref[2] = cand_terms
    offset_ref[...] = (
        updated
        - keep_rate * previous
        - reset_terms * recurrent[:, :width]
        - write_terms * recurrent[:, width : 2 * width]
        - cand_terms * cand_recurrent
    )

    def coupling(row):
        total = weight_ref[:, pl.ds(0, width)] * term_ref[0, pl.ds(row, 1), :]
        for part in (1, 2):
            columns = pl.ds(part * width, width)
            total = total + weight_ref[:, columns] * term_ref[part, pl.ds(row, 1), :]
        return total

    diagonal = lax.broadcasted_iota(jnp.int32, (width, width), 0) == lax.broadcasted_iota(
        jnp.int32, (width, width), 1
    )
    for block in range(blocks):
        row = block * BLOCK
        first = coupling(row) + jnp.where(diagonal, keep_ref[pl.ds(row, 1), :], 0.0)
        map_ref[block] = first

    def advance(states, now):
        mapped = few_rows(states, weight_parts, NN)
        states = keep_ref[now, :] * states + offset_ref[now, :]
        for part in range(3):
            columns = slice(part * width, (part + 1) * width)
            states = states + term_ref[part, now, :] * mapped[:, columns]
        return states

    def retreat(costates, now):
        spread = jnp.concatenate(
            [term_ref[part, now, :] * costates for part in range(3)], axis=1
        )
        return keep_ref[now, :] * costates + few_rows(spread, weight_parts, NT)

    def steps_at(step):
        return pl.ds(step, blocks, stride=BLOCK)

    def gather_step(step, carry):
        offsets, adjoints = carry
        for block in range(blocks):
            row = block * BLOCK + step
            mapped = map_ref[block]
            map_ref[block] = mapped * keep_ref[pl.ds(row, 1), :] + product(mapped, coupling(row))
        back = steps_at(BLOCK - step)
        return advance(offsets, steps_at(step)), retreat(cotan_ref[back, :] + adjoints, back)

    offsets, adjoints = lax.fori_loop(
        1,
        BLOCK,
        gather_step,
        (offset_ref[steps_at(0), :], jnp.zeros((blocks, width), jnp.float32)),
    )
    adjoints = retreat(cotan_ref[steps_at(0), :] + adjoints, steps_at(0))

    def repeated(rows, block):
        return jnp.broadcast_to(rows[block : block + 1], (PAD, width))

    levels = [
        [
            node_of(
                jnp.concatenate([map_ref[block], repeated(offsets, block)], axis=0),
                repeated(adjoints, block),
            )
            for block in range(blocks)
        ]
    ]
    while len(levels[-1]) > 1:
        nodes = levels[-1]
        levels.append([merge(nodes[i], nodes[i + 1]) for i in range(0, len(nodes), 2)])

    node = levels[-1][0]

    def write_message(target, node):
        target[pl.ds(0, width + SENT), :] = node[0][: width + SENT]
        target[pl.ds(width + SENT, SENT), :] = node[2][:SENT]

    def read_message(source):
        offset = source[pl.ds(width, SENT), :]
        adjoint = source[pl.ds(width + SENT, SENT), :]
        return node_of(
            jnp.concatenate([source[pl.ds(0, width), :], offset, offset], axis=0),
            jnp.concatenate([adjoint, adjoint], axis=0),
        )

    def copy_to(ref, index, partner):
        return pltpu.make_async_remote_copy(
            src_ref=ref,
            dst_ref=ref,
            send_sem=pair_send.at[index],
            recv_sem=pair_recv.at[index],
            device_id=at(partner),
        )

    def send(ref, index, partner):
        copy = copy_to(ref, index, partner)
        copy.start()
        return copy

    pairs = []
    write_message(pair_ref.at[0, sides[0]], node)
    sibling_copy = send(pair_ref.at[0, sides[0]], 0, partners[0])
    sibling_copy.wait_recv()
    pairs.append([read_message(pair_ref.at[0, i]) for i in (0, 1)])

    def pass_to(source, target, sems, distance):
        return [
            pltpu.make_async_remote_copy(
                src_ref=source,
                dst_ref=target,
                send_sem=sems.at[turn - 1],
                recv_sem=sems.at[2],
                device_id=at(me + distance * turn),
            )
            for turn in (1, 2)
        ]

    ahead_copies = pass_to(out_ahead_ref, ahead_ref, ahead_sems, GROUP)
    behind_copies = pass_to(out_behind_ref, behind_ref, behind_sems, -GROUP)
    entry_copy = pltpu.make_async_remote_copy(
        src_ref=entry_ref,
        dst_ref=entry_ref,
        send_sem=pair_send.at[2],
        recv_sem=pair_recv.at[2],
        device_id=at(partners[0]),
    )

    def doubled(rows):
        return jnp.concatenate([rows, rows], axis=0)

    @pl.when(sides[0] == 1)
    def _():
        write_message(pair_ref.at[1, sides[1]], merge(*pairs[0]))
        plane_copy = send(pair_ref.at[1, sides[1]], 1, partners[1])
        plane_copy.wait_recv()
        early, late = [read_message(pair_ref.at[1, i]) for i in (0, 1)]
        node = merge(early, late)

        write_message(pair_ref.at[2, odd], node)
        offsets_copy = copy_to(pair_ref.at[2, odd, pl.ds(width, 2 * SENT)], 3, neighbour)
        matrix_copy = copy_to(pair_ref.at[2, odd, pl.ds(0, width)], 4, neighbour)
        offsets_copy.start()

        @pl.when(1 - odd + after > 0)
        def _():
            matrix_copy.start()

        def pass_forward():
            @pl.when(couple == 0)
            def _():
                ahead_ref[...] = jnp.broadcast_to(initial_ref[...], ahead_ref.shape)

            @pl.when(couple > 0)
            def _():
                ahead_copies[0].wait_recv()

            @pl.when(odd == 1)
            def _():
                offsets_copy.wait_recv()
                matrix_copy.wait_recv()
                state = go_forward(read_message(pair_ref.at[2, 0]), doubled(ahead_ref[...]))
                ahead_ref[...] = state[:SENT]

                @pl.when(after > 0)
                def _():
                    out_ahead_ref[...] = go_forward(node, state)[:SENT]
                    for copy in ahead_copies:
                        copy.start()

        def pass_back():
            @pl.when(after > 0)
            def _():
                behind_copies[0].wait_recv()

            @pl.when(after == 0)
            def _():
                behind_ref[...] = jnp.zeros_like(behind_ref)

            @pl.when(odd == 0)
            def _():
                offsets_copy.wait_recv()

                @pl.when(after > 0)
                def _():
                    matrix_copy.wait_recv()
                    behind_ref[...] = go_back(
                        read_message(pair_ref.at[2, 1]), doubled(behind_ref[...])
                    )[:SENT]

                @pl.when(after == 0)
                def _():
                    behind_ref[...] = pair_ref[2, 1, pl.ds(width + SENT, SENT), :]

                @pl.when(couple > 0)
                def _():
                    out_behind_ref[...] = go_back(node, doubled(behind_ref[...]))[:SENT]
                    for copy in behind_copies:
                        copy.start()

        @pl.when(group < groups // 2)
        def _():
            pass_forward()
            pass_back()

        @pl.when(group >= groups // 2)
        def _():
            pass_back()
            pass_forward()

        state, costate = doubled(ahead_ref[...]), doubled(behind_ref[...])
        is_late = sides[1] == 1
        entry_ref[pl.ds(0, SENT), :] = jnp.where(is_late, go_forward(early, state), state)[:SENT]
        entry_ref[pl.ds(SENT, SENT), :] = jnp.where(is_late, costate, go_back(late, costate))[
            :SENT
        ]
        entry_copy.start()
        plane_copy.wait_send()
        offsets_copy.wait_send()

        @pl.when(1 - odd + after > 0)
        def _():
            matrix_copy.wait_send()

        @pl.when(odd * after > 0)
        def _():
            for copy in ahead_copies:
                copy.wait_send()

        @pl.when((1 - odd) * couple > 0)
        def _():
            for copy in behind_copies:
                copy.wait_send()

    @pl.when(sides[0] == 0)
    def _():
        entry_copy.wait_recv()

    state = doubled(entry_ref[pl.ds(0, SENT), :])
    costate = doubled(entry_ref[pl.ds(SENT, SENT), :])
    early, late = pairs[0]
    is_late = sides[0] == 1
    state, costate = (
        jnp.where(is_late, go_forward(early, state), state),
        jnp.where(is_late, costate, go_back(late, costate)),
    )

    entries = [(state, costate)]
    for nodes in reversed(levels[:-1]):
        finer = []
        for i, (state, costate) in enumerate(entries):
            early, late = nodes[2 * i], nodes[2 * i + 1]
            finer.append((state, go_back(late, costate)))
            finer.append((go_forward(early, state), costate))
        entries = finer

    states = jnp.concatenate([entry[0][:1] for entry in entries], axis=0)
    costates = jnp.concatenate([entry[1][:1] for entry in entries], axis=0)

    def apply_step(step, carry):
        states, costates = carry
        now, back = steps_at(step), steps_at(BLOCK - 1 - step)
        states = advance(states, now)
        state_out[now, :] = states
        costates = cotan_ref[back, :] + costates
        adjoint_out[back, :] = costates
        return states, retreat(costates, back)

    lax.fori_loop(0, BLOCK, apply_step, (states, costates))

    @pl.when(me < seq_count - 1)
    def _():
        row_copy.wait_send()

    sibling_copy.wait_send()

    @pl.when(sides[0] == 1)
    def _():
        entry_copy.wait_send()


def per_device(
    seq_count, inputs, trajectory, initial_state, cotangent, in_weight, recurrent_weight, gate_bias
):
    rows, width = trajectory.shape[1:]
    blocks = rows // BLOCK
    out = jax.ShapeDtypeStruct((rows, width), jnp.float32)
    vmem = functools.partial(pltpu.VMEM, dtype=jnp.float32)
    pair_sems = pltpu.SemaphoreType.DMA((2,))
    new_state, adjoint = pl.pallas_call(
        functools.partial(kernel, seq_count),
        out_shape=(out, out),
        in_specs=[pl.BlockSpec(memory_space=pltpu.HBM)] * 7,
        out_specs=(pl.BlockSpec(memory_space=pltpu.VMEM),) * 2,
        scratch_shapes=[
            vmem(inputs.shape[1:]),
            vmem((rows, width)),
            vmem((1, width)),
            vmem((rows, width)),
            vmem(in_weight.shape),
            vmem(recurrent_weight.shape),
            vmem((3 * width,)),
            pltpu.SemaphoreType.DMA((7,)),
            vmem((rows, width)),
            vmem((rows, width)),
            vmem((3, rows, width)),
            vmem((rows, width)),
            vmem((blocks, width, width)),
            vmem((len(GROUP_LEVELS) + 1, 2, width + 2 * SENT, width)),
            vmem((8, width)),
            vmem((SENT, width)),
            vmem((SENT, width)),
            vmem((SENT, width)),
            vmem((SENT, width)),
            vmem((2 * SENT, width)),
            pair_sems,
            pltpu.SemaphoreType.DMA((5,)),
            pltpu.SemaphoreType.DMA((5,)),
            pltpu.SemaphoreType.DMA((3,)),
            pltpu.SemaphoreType.DMA((3,)),
        ],
        compiler_params=pltpu.CompilerParams(
            collective_id=0, has_side_effects=True, vmem_limit_bytes=64 * 1024 * 1024
        ),
        name="newton_step",
    )(
        inputs[0],
        trajectory[0],
        initial_state,
        cotangent[0],
        in_weight,
        recurrent_weight,
        gate_bias,
    )
    return new_state[None], adjoint[None]


def solution(mesh):
    return jax.shard_map(
        functools.partial(per_device, mesh.shape["seq"]),
        mesh=mesh,
        in_specs=(
            P("dp", "seq", None),
            P("dp", "seq", None),
            P("dp", None),
            P("dp", "seq", None),
            P(),
            P(),
            P(),
        ),
        out_specs=(P("dp", "seq", None), P("dp", "seq", None)),
        check_vma=False,
    )
```

```python
import functools

import jax
import jax.numpy as jnp
from jax import lax
from jax.experimental import pallas as pl
from jax.experimental.pallas import tpu as pltpu
from jax.sharding import PartitionSpec as P

BLOCK = 8
GROUP_LEVELS = (1, 2)
GROUP = 4
PAD = 16
SENT = 8

NT = (((1,), (1,)), ((), ()))
NN = (((1,), (0,)), ((), ()))


def split(value):
    high = value.astype(jnp.bfloat16)
    low = (value - high.astype(jnp.float32)).astype(jnp.bfloat16)
    return high, low


def product_of_parts(rows, weights):
    (high, low), (w_high, w_low) = rows, weights
    width = w_high.shape[1]
    stacked = jnp.concatenate(
        [
            jnp.concatenate([w_high, w_low], axis=1),
            jnp.concatenate([w_high, jnp.zeros_like(w_low)], axis=1),
        ],
        axis=0,
    )
    out = jnp.dot(
        jnp.concatenate([high, low], axis=1), stacked, preferred_element_type=jnp.float32
    )
    return out[:, :width] + out[:, width:]


def product(rows, weights):
    return product_of_parts(split(rows), split(weights))


def few_rows(rows, parts, dims):
    count = rows.shape[0]
    side = 1 - dims[0][1][0]
    width = parts[0].shape[side]
    out = lax.dot_general(
        jnp.concatenate(split(rows), axis=0),
        jnp.concatenate(parts, axis=side),
        dims,
        preferred_element_type=jnp.float32,
    )
    return out[:count, :width] + out[count:, :width] + out[:count, width:]


def node_of(mapped, adjoint):
    return mapped, split(mapped), adjoint


def matrix_parts(node):
    width = node[0].shape[1]
    return tuple(part[:width] for part in node[1])


def merge(early, late):
    width = early[0].shape[1]
    merged = product_of_parts(early[1], matrix_parts(late))
    merged = jnp.concatenate([merged[:width], merged[width:] + late[0][width:]], axis=0)
    return node_of(merged, early[2] + few_rows(late[2], matrix_parts(early), NT))


def go_forward(node, state):
    return few_rows(state, matrix_parts(node), NN) + node[0][state.shape[1] :]


def go_back(node, costate):
    return few_rows(costate, matrix_parts(node), NT) + node[2]


def kernel(
    seq_count,
    features_hbm,
    path_hbm,
    initial_hbm,
    cotan_hbm,
    in_weight_hbm,
    weight_hbm,
    bias_hbm,
    state_out,
    adjoint_out,
    features_ref,
    path_ref,
    initial_ref,
    cotan_ref,
    in_weight_ref,
    weight_ref,
    bias_ref,
    fetch_sems,
    previous_ref,
    keep_ref,
    term_ref,
    offset_ref,
    map_ref,
    pair_ref,
    row_ref,
    ahead_ref,
    behind_ref,
    out_ahead_ref,
    out_behind_ref,
    entry_ref,
    row_sems,
    pair_send,
    pair_recv,
    ahead_sems,
    behind_sems,
):
    rows, width = path_hbm.shape
    blocks = rows // BLOCK
    me = lax.axis_index("seq")
    groups = seq_count // GROUP
    group = me // GROUP
    odd, couple = group % 2, group // 2
    after = groups // 2 - 1 - couple
    neighbour = me + GROUP - 2 * GROUP * odd

    def at(place):
        return {"seq": place}

    fetches = []
    for source, target in (
        (path_hbm, path_ref),
        (features_hbm, features_ref),
        (in_weight_hbm, in_weight_ref),
        (bias_hbm, bias_ref),
        (weight_hbm, weight_ref),
        (initial_hbm, initial_ref),
        (cotan_hbm, cotan_ref),
    ):
        fetch = pltpu.make_async_copy(source, target, fetch_sems.at[len(fetches)])
        fetch.start()
        fetches.append(fetch)

    barrier = pltpu.get_barrier_semaphore()
    greeted = jnp.int32(0)
    for distance in (1, GROUP, 2 * GROUP):

        @pl.when(me >= distance)
        def _():
            pl.semaphore_signal(barrier, inc=1, device_id=at(me - distance))

        @pl.when(me < seq_count - distance)
        def _():
            pl.semaphore_signal(barrier, inc=1, device_id=at(me + distance))

        greeted = greeted + jnp.where(me >= distance, 1, 0)
        greeted = greeted + jnp.where(me < seq_count - distance, 1, 0)
    sides = [(me // bit) % 2 for bit in GROUP_LEVELS]
    partners = [me + bit - 2 * bit * side for bit, side in zip(GROUP_LEVELS, sides)]
    for partner in partners[1:]:
        pl.semaphore_signal(barrier, inc=1, device_id=at(partner))
        greeted = greeted + 1
    pl.semaphore_wait(barrier, greeted)

    row_copy = pltpu.make_async_remote_copy(
        src_ref=path_hbm.at[pl.ds(rows - 8, 8)],
        dst_ref=row_ref,
        send_sem=row_sems.at[0],
        recv_sem=row_sems.at[1],
        device_id=at(me + 1),
    )

    @pl.when(me < seq_count - 1)
    def _():
        row_copy.start()

    for fetch in fetches[:4]:
        fetch.wait()

    projected = (
        product(features_ref[...], in_weight_ref[...])
        + bias_ref[...][None, :]
    )
    previous_ref[pl.ds(1, rows - 1), :] = path_ref[pl.ds(0, rows - 1), :]

    for fetch in fetches[4:]:
        fetch.wait()

    @pl.when(me > 0)
    def _():
        row_copy.wait_recv()
        previous_ref[pl.ds(0, 1), :] = row_ref[pl.ds(7, 1), :]

    @pl.when(me == 0)
    def _():
        previous_ref[pl.ds(0, 1), :] = initial_ref[...]

    previous = previous_ref[...]
    weight_parts = split(weight_ref[...])
    recurrent = product_of_parts(split(previous), weight_parts)
    reset_gate = jax.nn.sigmoid(projected[:, :width] + recurrent[:, :width])
    write_gate = jax.nn.sigmoid(
        projected[:, width : 2 * width] + recurrent[:, width : 2 * width]
    )
    cand_recurrent = recurrent[:, 2 * width :]
    candidate = jnp.tanh(projected[:, 2 * width :] + reset_gate * cand_recurrent)
    updated = previous + write_gate * (candidate - previous)
    keep_rate = 1.0 - write_gate
    slopes = write_gate * (1.0 - candidate * candidate)
    reset_terms = slopes * cand_recurrent * reset_gate * (1.0 - reset_gate)
    write_terms = (candidate - previous) * write_gate * (1.0 - write_gate)
    cand_terms = slopes * reset_gate
    keep_ref[...] = keep_rate
    term_ref[0] = reset_terms
    term_ref[1] = write_terms
    term_ref[2] = cand_terms
    offset_ref[...] = (
        updated
        - keep_rate * previous
        - reset_terms * recurrent[:, :width]
        - write_terms * recurrent[:, width : 2 * width]
        - cand_terms * cand_recurrent
    )

    def coupling(row):
        total = weight_ref[:, pl.ds(0, width)] * term_ref[0, pl.ds(row, 1), :]
        for part in (1, 2):
            columns = pl.ds(part * width, width)
            total = total + weight_ref[:, columns] * term_ref[part, pl.ds(row, 1), :]
        return total

    diagonal = lax.broadcasted_iota(jnp.int32, (width, width), 0) == lax.broadcasted_iota(
        jnp.int32, (width, width), 1
    )
    for block in range(blocks):
        row = block * BLOCK
        first = coupling(row) + jnp.where(diagonal, keep_ref[pl.ds(row, 1), :], 0.0)
        map_ref[block] = first

    def advance(states, now):
        mapped = few_rows(states, weight_parts, NN)
        states = keep_ref[now, :] * states + offset_ref[now, :]
        for part in range(3):
            columns = slice(part * width, (part + 1) * width)
            states = states + term_ref[part, now, :] * mapped[:, columns]
        return states

    def retreat(costates, now):
        spread = jnp.concatenate(
            [term_ref[part, now, :] * costates for part in range(3)], axis=1
        )
        return keep_ref[now, :] * costates + few_rows(spread, weight_parts, NT)

    def steps_at(step):
        return pl.ds(step, blocks, stride=BLOCK)

    def gather_step(step, carry):
        offsets, adjoints = carry
        for block in range(blocks):
            row = block * BLOCK + step
            mapped = map_ref[block]
            map_ref[block] = mapped * keep_ref[pl.ds(row, 1), :] + product(mapped, coupling(row))
        back = steps_at(BLOCK - step)
        return advance(offsets, steps_at(step)), retreat(cotan_ref[back, :] + adjoints, back)

    offsets, adjoints = lax.fori_loop(
        1,
        BLOCK,
        gather_step,
        (offset_ref[steps_at(0), :], jnp.zeros((blocks, width), jnp.float32)),
        unroll=True,
    )
    adjoints = retreat(cotan_ref[steps_at(0), :] + adjoints, steps_at(0))

    def repeated(rows, block):
        return jnp.broadcast_to(rows[block : block + 1], (PAD, width))

    levels = [
        [
            node_of(
                jnp.concatenate([map_ref[block], repeated(offsets, block)], axis=0),
                repeated(adjoints, block),
            )
            for block in range(blocks)
        ]
    ]
    while len(levels[-1]) > 1:
        nodes = levels[-1]
        levels.append([merge(nodes[i], nodes[i + 1]) for i in range(0, len(nodes), 2)])

    node = levels[-1][0]

    def write_message(target, node):
        target[pl.ds(0, width + SENT), :] = node[0][: width + SENT]
        target[pl.ds(width + SENT, SENT), :] = node[2][:SENT]

    def read_message(source):
        offset = source[pl.ds(width, SENT), :]
        adjoint = source[pl.ds(width + SENT, SENT), :]
        return node_of(
            jnp.concatenate([source[pl.ds(0, width), :], offset, offset], axis=0),
            jnp.concatenate([adjoint, adjoint], axis=0),
        )

    def copy_to(ref, index, partner):
        return pltpu.make_async_remote_copy(
            src_ref=ref,
            dst_ref=ref,
            send_sem=pair_send.at[index],
            recv_sem=pair_recv.at[index],
            device_id=at(partner),
        )

    def send(ref, index, partner):
        copy = copy_to(ref, index, partner)
        copy.start()
        return copy

    pairs = []
    write_message(pair_ref.at[0, sides[0]], node)
    sibling_copy = send(pair_ref.at[0, sides[0]], 0, partners[0])
    sibling_copy.wait_recv()
    pairs.append([read_message(pair_ref.at[0, i]) for i in (0, 1)])

    def pass_to(source, target, sems, distance):
        return [
            pltpu.make_async_remote_copy(
                src_ref=source,
                dst_ref=target,
                send_sem=sems.at[turn - 1],
                recv_sem=sems.at[2],
                device_id=at(me + distance * turn),
            )
            for turn in (1, 2)
        ]

    ahead_copies = pass_to(out_ahead_ref, ahead_ref, ahead_sems, GROUP)
    behind_copies = pass_to(out_behind_ref, behind_ref, behind_sems, -GROUP)
    entry_copy = pltpu.make_async_remote_copy(
        src_ref=entry_ref,
        dst_ref=entry_ref,
        send_sem=pair_send.at[2],
        recv_sem=pair_recv.at[2],
        device_id=at(partners[0]),
    )

    def doubled(rows):
        return jnp.concatenate([rows, rows], axis=0)

    @pl.when(sides[0] == 1)
    def _():
        write_message(pair_ref.at[1, sides[1]], merge(*pairs[0]))
        plane_copy = send(pair_ref.at[1, sides[1]], 1, partners[1])
        plane_copy.wait_recv()
        early, late = [read_message(pair_ref.at[1, i]) for i in (0, 1)]
        node = merge(early, late)

        write_message(pair_ref.at[2, odd], node)
        offsets_copy = copy_to(pair_ref.at[2, odd, pl.ds(width, 2 * SENT)], 3, neighbour)
        matrix_copy = copy_to(pair_ref.at[2, odd, pl.ds(0, width)], 4, neighbour)
        offsets_copy.start()

        @pl.when(1 - odd + after > 0)
        def _():
            matrix_copy.start()

        def pass_forward():
            @pl.when(couple == 0)
            def _():
                ahead_ref[...] = jnp.broadcast_to(initial_ref[...], ahead_ref.shape)

            @pl.when(couple > 0)
            def _():
                ahead_copies[0].wait_recv()

            @pl.when(odd == 1)
            def _():
                offsets_copy.wait_recv()
                matrix_copy.wait_recv()
                state = go_forward(read_message(pair_ref.at[2, 0]), doubled(ahead_ref[...]))
                ahead_ref[...] = state[:SENT]

                @pl.when(after > 0)
                def _():
                    out_ahead_ref[...] = go_forward(node, state)[:SENT]
                    for copy in ahead_copies:
                        copy.start()

        def pass_back():
            @pl.when(after > 0)
            def _():
                behind_copies[0].wait_recv()

            @pl.when(after == 0)
            def _():
                behind_ref[...] = jnp.zeros_like(behind_ref)

            @pl.when(odd == 0)
            def _():
                offsets_copy.wait_recv()

                @pl.when(after > 0)
                def _():
                    matrix_copy.wait_recv()
                    behind_ref[...] = go_back(
                        read_message(pair_ref.at[2, 1]), doubled(behind_ref[...])
                    )[:SENT]

                @pl.when(after == 0)
                def _():
                    behind_ref[...] = pair_ref[2, 1, pl.ds(width + SENT, SENT), :]

                @pl.when(couple > 0)
                def _():
                    out_behind_ref[...] = go_back(node, doubled(behind_ref[...]))[:SENT]
                    for copy in behind_copies:
                        copy.start()

        @pl.when(group < groups // 2)
        def _():
            pass_forward()
            pass_back()

        @pl.when(group >= groups // 2)
        def _():
            pass_back()
            pass_forward()

        state, costate = doubled(ahead_ref[...]), doubled(behind_ref[...])
        is_late = sides[1] == 1
        entry_ref[pl.ds(0, SENT), :] = jnp.where(is_late, go_forward(early, state), state)[:SENT]
        entry_ref[pl.ds(SENT, SENT), :] = jnp.where(is_late, costate, go_back(late, costate))[
            :SENT
        ]
        entry_copy.start()
        plane_copy.wait_send()
        offsets_copy.wait_send()

        @pl.when(1 - odd + after > 0)
        def _():
            matrix_copy.wait_send()

        @pl.when(odd * after > 0)
        def _():
            for copy in ahead_copies:
                copy.wait_send()

        @pl.when((1 - odd) * couple > 0)
        def _():
            for copy in behind_copies:
                copy.wait_send()

    @pl.when(sides[0] == 0)
    def _():
        entry_copy.wait_recv()

    state = doubled(entry_ref[pl.ds(0, SENT), :])
    costate = doubled(entry_ref[pl.ds(SENT, SENT), :])
    early, late = pairs[0]
    is_late = sides[0] == 1
    state, costate = (
        jnp.where(is_late, go_forward(early, state), state),
        jnp.where(is_late, costate, go_back(late, costate)),
    )

    entries = [(state, costate)]
    for nodes in reversed(levels[:-1]):
        finer = []
        for i, (state, costate) in enumerate(entries):
            early, late = nodes[2 * i], nodes[2 * i + 1]
            finer.append((state, go_back(late, costate)))
            finer.append((go_forward(early, state), costate))
        entries = finer

    states = jnp.concatenate([entry[0][:1] for entry in entries], axis=0)
    costates = jnp.concatenate([entry[1][:1] for entry in entries], axis=0)

    def apply_step(step, carry):
        states, costates = carry
        now, back = steps_at(step), steps_at(BLOCK - 1 - step)
        states = advance(states, now)
        state_out[now, :] = states
        costates = cotan_ref[back, :] + costates
        adjoint_out[back, :] = costates
        return states, retreat(costates, back)

    lax.fori_loop(0, BLOCK, apply_step, (states, costates))

    @pl.when(me < seq_count - 1)
    def _():
        row_copy.wait_send()

    sibling_copy.wait_send()

    @pl.when(sides[0] == 1)
    def _():
        entry_copy.wait_send()


def per_device(
    seq_count, inputs, trajectory, initial_state, cotangent, in_weight, recurrent_weight, gate_bias
):
    rows, width = trajectory.shape[1:]
    blocks = rows // BLOCK
    out = jax.ShapeDtypeStruct((rows, width), jnp.float32)
    vmem = functools.partial(pltpu.VMEM, dtype=jnp.float32)
    pair_sems = pltpu.SemaphoreType.DMA((2,))
    new_state, adjoint = pl.pallas_call(
        functools.partial(kernel, seq_count),
        out_shape=(out, out),
        in_specs=[pl.BlockSpec(memory_space=pltpu.HBM)] * 7,
        out_specs=(pl.BlockSpec(memory_space=pltpu.VMEM),) * 2,
        scratch_shapes=[
            vmem(inputs.shape[1:]),
            vmem((rows, width)),
            vmem((1, width)),
            vmem((rows, width)),
            vmem(in_weight.shape),
            vmem(recurrent_weight.shape),
            vmem((3 * width,)),
            pltpu.SemaphoreType.DMA((7,)),
            vmem((rows, width)),
            vmem((rows, width)),
            vmem((3, rows, width)),
            vmem((rows, width)),
            vmem((blocks, width, width)),
            vmem((len(GROUP_LEVELS) + 1, 2, width + 2 * SENT, width)),
            vmem((8, width)),
            vmem((SENT, width)),
            vmem((SENT, width)),
            vmem((SENT, width)),
            vmem((SENT, width)),
            vmem((2 * SENT, width)),
            pair_sems,
            pltpu.SemaphoreType.DMA((5,)),
            pltpu.SemaphoreType.DMA((5,)),
            pltpu.SemaphoreType.DMA((3,)),
            pltpu.SemaphoreType.DMA((3,)),
        ],
        compiler_params=pltpu.CompilerParams(
            collective_id=0, has_side_effects=True, vmem_limit_bytes=64 * 1024 * 1024
        ),
        name="newton_step",
    )(
        inputs[0],
        trajectory[0],
        initial_state,
        cotangent[0],
        in_weight,
        recurrent_weight,
        gate_bias,
    )
    return new_state[None], adjoint[None]


def solution(mesh):
    return jax.shard_map(
        functools.partial(per_device, mesh.shape["seq"]),
        mesh=mesh,
        in_specs=(
            P("dp", "seq", None),
            P("dp", "seq", None),
            P("dp", None),
            P("dp", "seq", None),
            P(),
            P(),
            P(),
        ),
        out_specs=(P("dp", "seq", None), P("dp", "seq", None)),
        check_vma=False,
    )
```
